32 devices in a mesh: ctx: 8 (over z, y), head: 4 (over x, core).
Axes of the slice: x: 2, y: 2, z: 4, core: 2. Of those that a mesh axis runs over, the one named last changes fastest.
Arguments:
- queries: bfloat16 [4096, 8192], P('ctx', 'head'), may hold values from -6 to 6
- keys: bfloat16 [4096, 8192], P('ctx', 'head'), may hold values from -6 to 6
- values: bfloat16 [4096, 8192], P('ctx', 'head'), may hold values from -6 to 6
- teacher: bfloat16 [4096, 5120], P('ctx', 'head'), may hold values from -6 to 6
- out_weight: bfloat16 [8192, 5120], P('head'), may hold values from -0.0625 to 0.0625
- valid: int32 [4096], P('ctx'), may hold values from 0 to 1, as said below
Outputs:
- q_grad: float32 [4096, 8192], P('ctx', 'head')
- k_grad: float32 [4096, 8192], P('ctx', 'head')
- v_grad: float32 [4096, 8192], P('ctx', 'head')
The draws below stay inside these ranges and needn't reach their ends.
Inputs may be any that keep to these rules, and one draw needn't show every extreme that they name: The last token always has valid = 1.
All inputs are finite; a program needn't handle non-finite values.
Results may differ from the reference program's by a relative error of at most 0.012.
Values may be sent and summed in bfloat16 or wider, within the bound.
No kernel may reach another device: no remote copies, remote signals or barrier semaphores. Data moves between devices by JAX's collectives and lax.ppermute only.
A program may use at most 128 MiB of HBM per device.

```python
import math
import jax
import jax.numpy as jnp
from jax import lax

H = 64
DH = 128
DM = 5120
HEADS_DEV = 16
TOKENS = 4096
N_HEAD = 4


def draw_valid(key, part):
    position = jnp.arange(TOKENS, dtype=jnp.int32)
    threshold = 256 + 512 * position // TOKENS
    rolled = jax.random.randint(jax.random.fold_in(key, 7), (TOKENS,), 0, 1024, dtype=jnp.int32)
    chosen = (rolled < threshold) | (position == TOKENS - 1)
    return jnp.where(chosen, 1, 0).astype(jnp.int32)


def level_of(own_key, shape, shards, low, top_value):
    def one(dim, blocks):
        steps = jax.random.uniform(jax.random.fold_in(jax.random.fold_in(own_key, 6), dim), (blocks,), jnp.float32, low / len(shards), top_value / len(shards))
        return jnp.repeat(jnp.exp(steps), shape[dim] // blocks).reshape((-1,) + (1,) * (len(shape) - dim - 1))

    level = one(*shards[0])
    for cut in shards[1:]:
        level = level * one(*cut)
    return level


def noise(key, dims, deviation, limit, shards=(), held_as=jnp.bfloat16):
    array = jax.random.normal(key, dims, jnp.float32) * deviation
    if len(shards) > 0:
        array = level_of(key, dims, shards, -0.22, 0.18) * array
    return jnp.clip(array, min=-limit, max=limit).astype(held_as)


def setup_inputs(seed: int = 0) -> dict:
    streams_of = jax.random.split(jax.random.key(seed), 7)
    queries = noise(streams_of[0], (TOKENS, H * DH), 1.0, 6.0, ((0, 8), (1, 4)))
    keys = noise(streams_of[1], (TOKENS, H * DH), 1.0, 6.0, ((0, 8), (1, 4)))
    values = noise(streams_of[2], (TOKENS, H * DH), 1.0, 6.0, ((0, 8), (1, 4)))
    teacher = noise(streams_of[3], (TOKENS, DM), 1.0, 6.0, ((0, 8), (1, 4)))
    out_weight = noise(streams_of[4], (H * DH, DM), (H * DH) ** -0.5, 0.0625, ((0, 4),))
    valid = draw_valid(jax.random.fold_in(streams_of[6], 71), 0)
    return dict(queries=queries, keys=keys, values=values, teacher=teacher, out_weight=out_weight, valid=valid)


def reference(queries, keys, values, teacher, out_weight, valid):
    precise = lax.Precision.HIGHEST
    attn_scale = 1.0 / math.sqrt(DH * TOKENS)
    blk_rows = math.gcd(TOKENS, 512)
    blk_count = TOKENS // blk_rows
    causal = jnp.tril(jnp.ones((blk_rows, blk_rows), jnp.float32))

    def attend(query_f, key_f, value_f):
        query_blk = query_f.reshape(blk_count, blk_rows, H, DH)
        key_blk = key_f.reshape(blk_count, blk_rows, H, DH)
        value_blk = value_f.reshape(blk_count, blk_rows, H, DH)

        def block_step(kv_state, inputs):
            query_one, key_one, value_one = inputs
            scores = jnp.einsum('thd,shd->hts', query_one, key_one, precision=precise) * causal
            output = jnp.einsum('hts,she->the', scores, value_one, precision=precise)
            output = output + jnp.einsum('thd,hde->the', query_one, kv_state, precision=precise)
            new_state = kv_state + jnp.einsum('thd,the->hde', key_one, value_one, precision=precise)
            return (new_state, output)
        zero_state = jnp.zeros((H, DH, DH), jnp.float32)
        final_state, outputs = lax.scan(block_step, zero_state, (query_blk, key_blk, value_blk))
        return attn_scale * outputs.reshape(TOKENS, H, DH)
    query_f = queries.astype(jnp.float32).reshape(TOKENS, H, DH)
    key_f = keys.astype(jnp.float32).reshape(TOKENS, H, DH)
    value_f = values.astype(jnp.float32).reshape(TOKENS, H, DH)
    attn_f, pullback = jax.vjp(attend, query_f, key_f, value_f)
    attn = attn_f.reshape(TOKENS, H * DH).astype(jnp.bfloat16)
    group_width = HEADS_DEV * DH
    predicted = jnp.zeros((TOKENS, DM), jnp.float32)
    for group_idx in range(N_HEAD):
        lower = group_idx * group_width
        partial_value = jnp.dot(attn[:, lower:lower + group_width], out_weight[lower:lower + group_width], preferred_element_type=jnp.float32)
        rounded = lax.optimization_barrier(partial_value.astype(jnp.bfloat16))
        predicted = predicted + rounded.astype(jnp.float32)
    valid_total = jnp.sum(valid).astype(jnp.float32)
    residual_err = predicted - teacher.astype(jnp.float32)
    error_grad = (valid.astype(jnp.float32)[:, None] * residual_err * (TOKENS / valid_total)).astype(jnp.bfloat16)
    attn_grad = jnp.dot(error_grad, out_weight.T, preferred_element_type=jnp.float32)
    q_grad, k_grad, v_grad = pullback(attn_grad.reshape(TOKENS, H, DH))
    return (q_grad.reshape(TOKENS, H * DH), k_grad.reshape(TOKENS, H * DH), v_grad.reshape(TOKENS, H * DH))
```

```python
import functools
import math

import jax
import jax.numpy as jnp
from jax import lax
from jax.experimental import pallas as pl
from jax.experimental.pallas import tpu as pltpu
from jax.sharding import PartitionSpec as P

DH = 128
PAIR = 2
VMEM_LIMIT = 40 * 1024 * 1024
NT = (((1,), (1,)), ((), ()))
TN = (((0,), (0,)), ((), ()))
F32 = jnp.float32
BF16 = jnp.bfloat16


def dot(a, b, dims=(((1,), (0,)), ((), ()))):
    return lax.dot_general(a, b, dims, preferred_element_type=F32)


def call(body, grid, in_specs, out_specs, out_shape, flops, moved, aliases=None):
    return pl.pallas_call(
        body,
        grid_spec=pltpu.PrefetchScalarGridSpec(
            num_scalar_prefetch=1, grid=grid, in_specs=in_specs, out_specs=out_specs
        ),
        out_shape=out_shape,
        input_output_aliases=aliases or {},
        compiler_params=pltpu.CompilerParams(vmem_limit_bytes=VMEM_LIMIT),
        cost_estimate=pl.CostEstimate(flops=flops, bytes_accessed=moved, transcendentals=0),
    )


def sds(shape, dtype):
    return jax.ShapeDtypeStruct(shape, dtype)


def lower_mask(n):
    rows = lax.broadcasted_iota(jnp.int32, (n, n), 0)
    cols = lax.broadcasted_iota(jnp.int32, (n, n), 1)
    return rows >= cols


def kv_body(idx, k, v, out):
    for i in range(PAIR):
        c = slice(i * DH, (i + 1) * DH)
        out[i] = dot(k[:, c], v[:, c], TN).astype(BF16)


def kv_states(half, k, v, half_heads):
    rows = k.shape[0]
    steps = half_heads // PAIR
    blk = pl.BlockSpec((rows, PAIR * DH), lambda i, s: (0, s[0] * steps + i))
    return call(
        kv_body,
        (steps,),
        [blk, blk],
        pl.BlockSpec((PAIR, DH, DH), lambda i, s: (i, 0, 0)),
        sds((half_heads, DH, DH), BF16),
        2 * rows * DH * DH * half_heads,
        rows * DH * half_heads * 4,
    )(half, k, v)


def intra_body(block, idx, q, k, v, out):
    mask = lower_mask(block)
    n = q.shape[0] // block
    for i in range(PAIR):
        c = slice(i * DH, (i + 1) * DH)
        state = None
        for b in range(n):
            r = slice(b * block, (b + 1) * block)
            qb, kb, vb = q[r, c], k[r, c], v[r, c]
            s = jnp.where(mask, dot(qb, kb, NT), 0.0).astype(BF16)
            o = dot(s, vb)
            if state is not None:
                o = o + dot(qb, state.astype(BF16))
            if b < n - 1:
                kv = dot(kb, vb, TN)
                state = kv if state is None else state + kv
            out[r, c] = o


def intra(half, q, k, v, half_heads):
    rows = k.shape[0]
    block = math.gcd(rows, 256)
    steps = half_heads // PAIR
    blk = pl.BlockSpec((rows, PAIR * DH), lambda i, s: (0, s[0] * steps + i))
    return call(
        functools.partial(intra_body, block),
        (steps,),
        [blk, blk, blk],
        pl.BlockSpec((rows, PAIR * DH), lambda i, s: (0, i)),
        sds((rows, half_heads * DH), F32),
        4 * rows * (block + DH) * DH * half_heads,
        rows * DH * half_heads * 10,
    )(half, q, k, v)


def attn_body(scale, idx, q, part, state, out):
    for i in range(PAIR):
        c = slice(i * DH, (i + 1) * DH)
        out[:, c] = (scale * (part[:, c] + dot(q[:, c], state[i]))).astype(BF16)


def attend(half, scale, q, part, state, half_heads):
    rows = q.shape[0]
    steps = half_heads // PAIR
    return call(
        functools.partial(attn_body, scale),
        (steps,),
        [
            pl.BlockSpec((rows, PAIR * DH), lambda i, s: (0, s[0] * steps + i)),
            pl.BlockSpec((rows, PAIR * DH), lambda i, s: (0, i)),
            pl.BlockSpec((PAIR, DH, DH), lambda i, s: (i, 0, 0)),
        ],
        pl.BlockSpec((rows, PAIR * DH), lambda i, s: (0, i)),
        sds((rows, half_heads * DH), BF16),
        2 * rows * DH * DH * half_heads,
        rows * DH * half_heads * 8,
    )(half, q, part, state)


def project_body(idx, a0, a1, w0, w1, out):
    out[...] = (dot(a0[...], w0[...]) + dot(a1[...], w1[...])).astype(BF16)


def project(idx, a0, a1, weight, tile, tiles):
    rows, depth = a0.shape
    return call(
        project_body,
        (tiles,),
        [
            pl.BlockSpec((rows, depth), lambda i, s: (0, 0)),
            pl.BlockSpec((rows, depth), lambda i, s: (0, 0)),
            pl.BlockSpec((depth, tile), lambda i, s: (s[0], s[2] + i)),
            pl.BlockSpec((depth, tile), lambda i, s: (s[1], s[2] + i)),
        ],
        pl.BlockSpec((rows, tile), lambda i, s: (0, i)),
        sds((rows, tiles * tile), BF16),
        4 * rows * depth * tile * tiles,
        4 * depth * tile * tiles + 4 * rows * depth + 2 * rows * tile * tiles,
    )(idx, a0, a1, weight, weight)


def grad_body(groups, with_acc, spans, idx, *refs):
    refs = list(refs)
    acc = refs.pop(0)[...] if with_acc else None
    out = refs.pop()
    for _ in range(groups):
        pieces = [refs.pop(0) for _ in spans]
        w = refs.pop(0)
        for piece, (lo, hi) in zip(pieces, spans):
            t = dot(piece[...], w[:, lo:hi], NT)
            acc = t if acc is None else acc + t
    out[...] = acc


def grad_accumulate(idx, groups, acc, spans, weight, width, row_tile):
    depth = weight.shape[0]
    rows = groups[0][0].shape[0]
    in_specs, args = [], []
    if acc is not None:
        in_specs.append(pl.BlockSpec((rows, row_tile), lambda i, s: (0, i)))
        args.append(acc)
    total = 0
    for g, pieces in enumerate(groups):
        for piece in pieces:
            in_specs.append(pl.BlockSpec(piece.shape, lambda i, s: (0, 0)))
            args.append(piece)
            total += piece.shape[1]
        in_specs.append(pl.BlockSpec((row_tile, width), lambda i, s, g=g: (i, s[g])))
        args.append(weight)
    return call(
        functools.partial(grad_body, len(groups), acc is not None, spans),
        (depth // row_tile,),
        in_specs,
        pl.BlockSpec((rows, row_tile), lambda i, s: (0, i)),
        sds((rows, depth), F32),
        2 * rows * depth * total,
        2 * depth * total + 8 * rows * depth,
        {1: 0} if acc is not None else None,
    )(idx, *args)


def last_body(groups, idx, acc, q, *refs):
    *refs, g_out, r_out = refs
    t = acc[...]
    for n in range(groups):
        t = t + dot(refs[2 * n][...], refs[2 * n + 1][...], NT)
    g = t.astype(BF16)
    g_out[...] = g
    for i in range(PAIR):
        c = slice(i * DH, (i + 1) * DH)
        r_out[i] = dot(q[:, c], g[:, c], TN).astype(BF16)


def grad_last(idx, acc, q, pieces, weight, half_heads):
    rows, tile = pieces[0].shape
    steps = half_heads // PAIR
    wide = PAIR * DH
    mine = pl.BlockSpec((rows, wide), lambda i, s: (0, s[0] * steps + i))
    in_specs, args = [mine, mine], [acc, q]
    for n, piece in enumerate(pieces):
        in_specs.append(pl.BlockSpec(piece.shape, lambda i, s: (0, 0)))
        in_specs.append(pl.BlockSpec((wide, tile), lambda i, s, n=n: (s[0] * steps + i, s[1 + n])))
        args += [piece, weight]
    return call(
        functools.partial(last_body, len(pieces)),
        (steps,),
        in_specs,
        [
            pl.BlockSpec((rows, wide), lambda i, s: (0, i)),
            pl.BlockSpec((PAIR, DH, DH), lambda i, s: (i, 0, 0)),
        ],
        [sds((rows, half_heads * DH), BF16), sds((half_heads, DH, DH), BF16)],
        2 * rows * half_heads * DH * (tile * len(pieces) + DH),
        half_heads * DH * (rows * 8 + 2 * tile * len(pieces)),
    )(idx, *args)


def back_body(block, scale, extra, idx, q, k, v, g, state, *refs):
    dq, dk, dv = refs[extra:]
    mask = lower_mask(block)
    n = q.shape[0] // block
    for i in range(PAIR):
        c = slice(i * DH, (i + 1) * DH)
        before = state[i].astype(F32)
        later = None
        dks, dvs = [], []
        for b in range(n):
            r = slice(b * block, (b + 1) * block)
            qb, kb, vb, gb = q[r, c], k[r, c], v[r, c], g[r, c]
            gs = jnp.where(mask, dot(gb, vb, NT), 0.0).astype(BF16)
            s = jnp.where(mask, dot(qb, kb, NT), 0.0).astype(BF16)
            dq[r, c] = scale * (dot(gs, kb) + dot(gb, before.astype(BF16), NT))
            dks.append(dot(gs, qb, TN))
            dvs.append(dot(s, gb, TN))
            if b < n - 1:
                before = before + dot(kb, vb, TN)
        for b in reversed(range(n)):
            r = slice(b * block, (b + 1) * block)
            qb, kb, vb, gb = q[r, c], k[r, c], v[r, c], g[r, c]
            dkb, dvb = dks[b], dvs[b]
            if later is not None:
                lb = later.astype(BF16)
                dkb = dkb + dot(vb, lb, NT)
                dvb = dvb + dot(kb, lb)
            dk[r, c] = scale * dkb
            dv[r, c] = scale * dvb
            if b > 0:
                qg = dot(qb, gb, TN)
                later = qg if later is None else later + qg


def back_local(half, scale, q, k, v, g, state, filled, half_heads):
    rows, width = q.shape
    block = math.gcd(rows, 256)
    steps = half_heads // PAIR
    wide = PAIR * DH
    mine = pl.BlockSpec((rows, wide), lambda i, s: (0, s[0] * steps + i))
    extra = len(filled)
    return call(
        functools.partial(back_body, block, scale, extra),
        (steps,),
        [
            mine,
            mine,
            mine,
            pl.BlockSpec((rows, wide), lambda i, s: (0, i)),
            pl.BlockSpec((PAIR, DH, DH), lambda i, s: (i, 0, 0)),
        ]
        + [pl.BlockSpec(memory_space=pl.ANY)] * extra,
        [mine] * 3,
        [sds((rows, width), F32)] * 3,
        2 * rows * DH * (5 * block + 4 * DH) * half_heads,
        rows * DH * half_heads * 20,
        {6 + n: n for n in range(extra)},
    )(half, q, k, v, g, state, *filled)


def later_body(scale, idx, k, v, later, dk_in, dv_in, dk, dv):
    for i in range(PAIR):
        c = slice(i * DH, (i + 1) * DH)
        dk[:, c] = dk_in[:, c] + scale * dot(v[:, c], later[i], NT)
        dv[:, c] = dv_in[:, c] + scale * dot(k[:, c], later[i])


def add_later(half, scale, k, v, later, dk, dv, half_heads):
    rows, width = k.shape
    steps = half_heads // PAIR
    mine = pl.BlockSpec((rows, PAIR * DH), lambda i, s: (0, s[0] * steps + i))
    return call(
        functools.partial(later_body, scale),
        (steps,),
        [mine, mine, pl.BlockSpec((PAIR, DH, DH), lambda i, s: (i, 0, 0)), mine, mine],
        [mine, mine],
        [sds((rows, width), F32)] * 2,
        4 * rows * DH * DH * half_heads,
        rows * DH * half_heads * 20,
        {4: 0, 5: 1},
    )(half, k, v, later, dk, dv)


def swap(array, axis, bit):
    size = lax.axis_size(axis)
    return lax.ppermute(array, axis, [(i, i ^ (1 << bit)) for i in range(size)])


def scan_states(theirs, mine, ctx_bits, flipped):
    pos = lax.axis_index("ctx")
    if flipped:
        pos = lax.axis_size("ctx") - 1 - pos
    own = mine.astype(F32)
    got = swap(theirs, "ctx", 0).astype(F32)
    total = own + got
    prefix = jnp.zeros_like(total)
    for bit in range(1, ctx_bits):
        other = swap(total.astype(BF16), "ctx", bit).astype(F32)
        prefix = prefix + jnp.where((pos >> bit) & 1 == 1, other, 0.0)
        total = total + other
    upper = pos & 1 == 1
    mine_prefix = (prefix + jnp.where(upper, got, 0.0)).astype(BF16)
    sent = (prefix + jnp.where(upper, 0.0, own)).astype(BF16)
    return mine_prefix, swap(sent, "ctx", 0)


def on_device(queries, keys, values, teacher, out_weight, valid):
    rows, width = queries.shape
    heads = width // DH
    half_heads = heads // 2
    ctx_size = lax.axis_size("ctx")
    ctx_bits = ctx_size.bit_length() - 1
    chips = lax.axis_size("head") // 2
    ctx_id, head_id = lax.axis_index("ctx"), lax.axis_index("head")
    chip, core = head_id // 2, head_id % 2
    scale = 1.0 / math.sqrt(DH * rows * ctx_size)
    piece_width = teacher.shape[1]
    tile = 256 if piece_width % 256 == 0 else 128
    tiles = piece_width // tile
    cuts = [0, 1, tiles - 1, tiles] if tiles > 2 else list(range(tiles + 1))
    spans = [(lo * tile, hi * tile) for lo, hi in zip(cuts[:-1], cuts[1:])]

    my_half = ctx_id & 1
    mine_ix = my_half[None].astype(jnp.int32)
    theirs_ix = 1 - mine_ix

    count = jnp.full((8, 128), jnp.sum(valid), jnp.int32)

    kv_theirs = kv_states(theirs_ix, keys, values, half_heads)
    kv_mine = kv_states(mine_ix, keys, values, half_heads)
    before_mine, before_theirs = scan_states(kv_theirs, kv_mine, ctx_bits, False)
    part_mine = intra(mine_ix, queries, keys, values, half_heads)
    part_theirs = intra(theirs_ix, queries, keys, values, half_heads)
    attn_mine = attend(mine_ix, scale, queries, part_mine, before_mine, half_heads)
    attn_theirs = attend(theirs_ix, scale, queries, part_theirs, before_theirs, half_heads)

    for bit in range(ctx_bits):
        count = count + swap(count, "ctx", bit)
    factor = rows * ctx_size / count[0, 0].astype(F32)
    weigh = (valid.astype(F32) * factor)[:, None]

    def column_tile(to_chip, to_core, lo):
        return (to_chip * 2 + to_core) * tiles + lo // tile

    def terms(to_chip, to_core, lo, hi):
        idx = jnp.stack([my_half, 1 - my_half, column_tile(to_chip, to_core, lo)])
        return project(
            idx.astype(jnp.int32), attn_mine, attn_theirs, out_weight, tile, (hi - lo) // tile
        )

    def shift(array, by):
        size = 2 * chips
        return lax.ppermute(array, "head", [(i, (i + 2 * by) % size) for i in range(size)])

    arrived = []
    for lo, hi in spans:
        got = []
        for by in range(1, chips):
            to_chip = lax.rem(chip + by, chips)
            away = terms(to_chip, 1 - core, lo, hi)
            kept = terms(to_chip, core, lo, hi)
            summed = kept.astype(F32) + swap(away, "head", 0).astype(F32)
            got.append(shift(summed.astype(BF16), by))
        arrived.append(got)
    away = terms(chip, 1 - core, 0, piece_width)
    kept = terms(chip, core, 0, piece_width)
    other_core = swap(away, "head", 0)

    errors = []
    for (lo, hi), got in zip(spans, arrived):
        predicted = kept[:, lo:hi].astype(F32) + other_core[:, lo:hi].astype(F32)
        for piece in got:
            predicted = predicted + piece.astype(F32)
        errors.append((weigh * (predicted - teacher[:, lo:hi].astype(F32))).astype(BF16))

    gathered = [[shift(error, by) for by in range(1, chips)] for error in errors]
    near = [errors, [swap(error, "head", 0) for error in errors]]
    row_tile = PAIR * DH
    idx = jnp.stack([chip * 2 + core, chip * 2 + 1 - core]).astype(jnp.int32)
    acc = grad_accumulate(idx, near, None, spans, out_weight, piece_width, row_tile)

    far, far_ix, last, last_ix = [], [], [], [theirs_ix[0]]
    for by in range(1, chips):
        from_chip = lax.rem(chip + chips - by, chips)
        pieces = [got[by - 1] for got in gathered]
        crossed = [swap(piece, "head", 0) for piece in pieces]
        for from_core, group in ((core, pieces), (1 - core, crossed)):
            far.append(group[:-1])
            far_ix.append(from_chip * 2 + from_core)
            last.append(group[-1])
            last_ix.append(column_tile(from_chip, from_core, spans[-1][0]))
    if far:
        acc = grad_accumulate(
            jnp.stack(far_ix).astype(jnp.int32),
            far, acc, spans[:-1], out_weight, piece_width, row_tile,
        )
    last_ix = jnp.stack(last_ix).astype(jnp.int32)
    g_theirs, r_theirs = grad_last(last_ix, acc, queries, last, out_weight, half_heads)
    g_mine, r_mine = grad_last(
        last_ix.at[0].set(mine_ix[0]), acc, queries, last, out_weight, half_heads
    )
    later_mine, later_theirs = scan_states(r_theirs, r_mine, ctx_bits, True)

    grads = back_local(
        theirs_ix, scale, queries, keys, values, g_theirs, before_theirs, [], half_heads
    )
    q_grad, k_grad, v_grad = back_local(
        mine_ix, scale, queries, keys, values, g_mine, before_mine, grads, half_heads
    )
    k_grad, v_grad = add_later(
        mine_ix, scale, keys, values, later_mine, k_grad, v_grad, half_heads
    )
    k_grad, v_grad = add_later(
        theirs_ix, scale, keys, values, later_theirs, k_grad, v_grad, half_heads
    )
    return q_grad, k_grad, v_grad


def solution(mesh):
    in_specs = (
        P("ctx", "head"),
        P("ctx", "head"),
        P("ctx", "head"),
        P("ctx", "head"),
        P("head", None),
        P("ctx"),
    )
    out_specs = (P("ctx", "head"), P("ctx", "head"), P("ctx", "head"))
    return jax.shard_map(
        on_device, mesh=mesh, in_specs=in_specs, out_specs=out_specs, check_vma=False
    )
```

```python
import functools
import math

import jax
import jax.numpy as jnp
from jax import lax
from jax.experimental import pallas as pl
from jax.experimental.pallas import tpu as pltpu
from jax.sharding import PartitionSpec as P

DH = 128
GROUP = 4
HINT = 1000000000000
NT = (((1,), (1,)), ((), ()))
TN = (((0,), (0,)), ((), ()))
F32 = jnp.float32
BF16 = jnp.bfloat16


def dot(a, b, dims=(((1,), (0,)), ((), ()))):
    return lax.dot_general(a, b, dims, preferred_element_type=F32)


def call(body, grid, in_specs, out_specs, out_shape, flops, moved, aliases=None, after=(), vmem=40, scratch=(), token=False):
    count = len(in_specs)
    if token:
        out_specs = [*out_specs, pl.BlockSpec((8, 128), lambda *_: (0, 0))]
        out_shape = [*out_shape, sds((8, 128), F32)]

    def ordered(idx, *refs):
        refs = list(refs)
        if token:
            refs.pop(count + len(after) + len(out_shape) - 1)[...] = jnp.zeros((8, 128), F32)
        body(idx, *refs[:count], *refs[count + len(after) :])

    kernel = pl.pallas_call(
        ordered,
        grid_spec=pltpu.PrefetchScalarGridSpec(
            num_scalar_prefetch=1,
            grid=grid,
            in_specs=list(in_specs) + [pl.BlockSpec(memory_space=pl.ANY)] * len(after),
            out_specs=out_specs,
            scratch_shapes=list(scratch),
        ),
        out_shape=out_shape,
        input_output_aliases=aliases or {},
        compiler_params=pltpu.CompilerParams(vmem_limit_bytes=vmem * 1024 * 1024),
        cost_estimate=pl.CostEstimate(
            flops=max(1, flops // HINT), bytes_accessed=max(1, moved // HINT), transcendentals=0
        ),
    )
    return lambda *args: kernel(*args, *after)


def sds(shape, dtype):
    return jax.ShapeDtypeStruct(shape, dtype)


def lower_mask(n):
    rows = lax.broadcasted_iota(jnp.int32, (n, n), 0)
    cols = lax.broadcasted_iota(jnp.int32, (n, n), 1)
    return rows >= cols


def cut(i):
    return slice(i * DH, (i + 1) * DH)


def group_of(half_heads):
    return math.gcd(half_heads, GROUP)


def kv_body(group, idx, k, v, out):
    for i in range(group):
        out[i] = dot(k[:, cut(i)], v[:, cut(i)], TN).astype(BF16)


def kv_states(half, k, v, half_heads, after=()):
    rows = k.shape[0]
    group = group_of(half_heads)
    steps = half_heads // group
    blk = pl.BlockSpec((rows, group * DH), lambda i, s: (0, s[0] * steps + i))
    return call(
        functools.partial(kv_body, group),
        (steps,),
        [blk, blk],
        pl.BlockSpec((group, DH, DH), lambda i, s: (i, 0, 0)),
        sds((half_heads, DH, DH), BF16),
        2 * rows * DH * DH * half_heads,
        rows * DH * half_heads * 4,
        after=after,
        vmem=58,
    )(half, k, v)


def intra_body(group, block, idx, q, k, v, out):
    mask = lower_mask(block)
    n = q.shape[0] // block
    for i in range(group):
        c = cut(i)
        state = None
        for b in range(n):
            r = slice(b * block, (b + 1) * block)
            qb, kb, vb = q[r, c], k[r, c], v[r, c]
            s = jnp.where(mask, dot(qb, kb, NT), 0.0).astype(BF16)
            o = dot(s, vb)
            if state is not None:
                o = o + dot(qb, state.astype(BF16))
            if b < n - 1:
                kv = dot(kb, vb, TN)
                state = kv if state is None else state + kv
            out[r, c] = o


def intra(half, q, k, v, half_heads, after):
    rows = k.shape[0]
    block = math.gcd(rows, 256)
    group = group_of(half_heads)
    steps = half_heads // group
    blk = pl.BlockSpec((rows, group * DH), lambda i, s: (0, s[0] * steps + i))
    return call(
        functools.partial(intra_body, group, block),
        (steps,),
        [blk, blk, blk],
        pl.BlockSpec((rows, group * DH), lambda i, s: (0, i)),
        sds((rows, half_heads * DH), F32),
        4 * rows * (block + DH) * DH * half_heads,
        rows * DH * half_heads * 10,
        after=after,
        vmem=58,
    )(half, q, k, v)


def attn_body(group, scale, idx, q, part, state, out):
    for i in range(group):
        c = cut(i)
        out[:, c] = (scale * (part[:, c] + dot(q[:, c], state[i]))).astype(BF16)


def attend(half, scale, q, part, state, half_heads):
    rows = q.shape[0]
    group = group_of(half_heads)
    steps = half_heads // group
    blk = pl.BlockSpec((rows, group * DH), lambda i, s: (0, i))
    return call(
        functools.partial(attn_body, group, scale),
        (steps,),
        [
            pl.BlockSpec((rows, group * DH), lambda i, s: (0, s[0] * steps + i)),
            blk,
            pl.BlockSpec((group, DH, DH), lambda i, s: (i, 0, 0)),
        ],
        blk,
        sds((rows, half_heads * DH), BF16),
        2 * rows * DH * DH * half_heads,
        rows * DH * half_heads * 8,
    )(half, q, part, state)


def project_body(idx, a0, b0, a1, b1, w, wo, out, acc):
    i = pl.program_id(0)

    @pl.when(i == 0)
    def _():
        acc[...] = dot(a0[...], w[...]) + dot(b0[...], wo[...])

    @pl.when(i == 1)
    def _():
        out[...] = (acc[...] + dot(a1[...], w[...]) + dot(b1[...], wo[...])).astype(BF16)


def project(idx, mine, theirs, weight, other_weight, span, after=()):
    rows, depth = mine[0].shape
    whole = pl.BlockSpec((rows, depth), lambda i, s: (0, 0))
    return call(
        project_body,
        (2,),
        [
            whole,
            whole,
            whole,
            whole,
            pl.BlockSpec(
                (pl.Element(depth), pl.Element(span)), lambda i, s: (s[i] * depth, s[2] * 128)
            ),
            pl.BlockSpec(
                (pl.Element(depth), pl.Element(span)), lambda i, s: (s[i] * depth, s[2] * 128)
            ),
        ],
        pl.BlockSpec((rows, span), lambda i, s: (0, 0)),
        sds((rows, span), BF16),
        8 * rows * depth * span,
        8 * depth * span + 8 * rows * depth + 2 * rows * span,
        after=after,
        vmem=44,
        scratch=[pltpu.VMEM((rows, span), F32)],
    )(idx, *mine, *theirs, weight, other_weight)


def grad_body(groups, with_acc, spans, idx, *refs):
    refs = list(refs)
    acc = refs.pop(0)[...] if with_acc else None
    out = refs.pop()
    for _ in range(groups):
        pieces = [refs.pop(0) for _ in spans]
        w = refs.pop(0)
        for piece, (lo, hi) in zip(pieces, spans):
            t = dot(piece[...], w[:, lo:hi], NT)
            acc = t if acc is None else acc + t
    out[...] = acc


def grad_accumulate(idx, groups, acc, spans, weight, width, after=()):
    depth = weight.shape[0]
    rows = groups[0][0].shape[0]
    row_tile = math.gcd(depth, 512)
    in_specs, args = [], []
    if acc is not None:
        in_specs.append(pl.BlockSpec((rows, row_tile), lambda i, s: (0, i)))
        args.append(acc)
    total = 0
    for g, pieces in enumerate(groups):
        for piece in pieces:
            in_specs.append(pl.BlockSpec(piece.shape, lambda i, s: (0, 0)))
            args.append(piece)
            total += piece.shape[1]
        in_specs.append(pl.BlockSpec((row_tile, width), lambda i, s, g=g: (i, s[g])))
        args.append(weight)
    return call(
        functools.partial(grad_body, len(groups), acc is not None, spans),
        (depth // row_tile,),
        in_specs,
        [pl.BlockSpec((rows, row_tile), lambda i, s: (0, i))],
        [sds((rows, depth), F32)],
        2 * rows * depth * total,
        2 * depth * total + 8 * rows * depth,
        {1: 0} if acc is not None else None,
        after=after,
        vmem=58,
        token=True,
    )(idx, *args)


def last_body(group, counts, idx, acc, q, *refs):
    *refs, g_out, r_out = refs
    t = acc[...]
    for count in counts:
        w, lo = refs[count], 0
        for piece in refs[:count]:
            hi = lo + piece.shape[1]
            t = t + dot(piece[...], w[:, lo:hi], NT)
            lo = hi
        refs = refs[count + 1 :]
    g = t.astype(BF16)
    g_out[...] = g
    for i in range(group):
        r_out[i] = dot(q[:, cut(i)], g[:, cut(i)], TN).astype(BF16)


def grad_last(idx, acc, q, groups, weight, half_heads, after=()):
    rows = acc.shape[0]
    group = group_of(half_heads)
    steps = half_heads // group
    wide = group * DH
    mine = pl.BlockSpec((rows, wide), lambda i, s: (0, s[0] * steps + i))
    in_specs, args, total = [mine, mine], [acc, q], 0
    for n, pieces in enumerate(groups):
        span = sum(piece.shape[1] for piece in pieces)
        total += span
        in_specs += [pl.BlockSpec(piece.shape, lambda i, s: (0, 0)) for piece in pieces]
        in_specs.append(
            pl.BlockSpec(
                (pl.Element(wide), pl.Element(span)),
                lambda i, s, n=n: ((s[0] * steps + i) * wide, s[1 + n] * 128),
            )
        )
        args += pieces + [weight]
    return call(
        functools.partial(last_body, group, [len(pieces) for pieces in groups]),
        (steps,),
        in_specs,
        [
            pl.BlockSpec((rows, wide), lambda i, s: (0, i)),
            pl.BlockSpec((group, DH, DH), lambda i, s: (i, 0, 0)),
        ],
        [sds((rows, half_heads * DH), BF16), sds((half_heads, DH, DH), BF16)],
        2 * rows * half_heads * DH * (total + DH),
        half_heads * DH * (rows * 8 + 2 * total),
        after=after,
        vmem=58,
    )(idx, *args)


def back_body(group, block, scale, extra, idx, q, k, v, g, state, *refs):
    dq, dk, dv = refs[extra:]
    mask = lower_mask(block)
    n = q.shape[0] // block
    for i in range(group):
        c = cut(i)
        before = state[i].astype(F32)
        later = None
        dks, dvs = [], []
        for b in range(n):
            r = slice(b * block, (b + 1) * block)
            qb, kb, vb, gb = q[r, c], k[r, c], v[r, c], g[r, c]
            gs = jnp.where(mask, dot(gb, vb, NT), 0.0).astype(BF16)
            s = jnp.where(mask, dot(qb, kb, NT), 0.0).astype(BF16)
            dq[r, c] = scale * (dot(gs, kb) + dot(gb, before.astype(BF16), NT))
            dks.append(dot(gs, qb, TN))
            dvs.append(dot(s, gb, TN))
            if b < n - 1:
                before = before + dot(kb, vb, TN)
        for b in reversed(range(n)):
            r = slice(b * block, (b + 1) * block)
            qb, kb, vb, gb = q[r, c], k[r, c], v[r, c], g[r, c]
            dkb, dvb = dks[b], dvs[b]
            if later is not None:
                lb = later.astype(BF16)
                dkb = dkb + dot(vb, lb, NT)
                dvb = dvb + dot(kb, lb)
            dk[r, c] = dkb
            dv[r, c] = dvb
            if b > 0:
                qg = dot(qb, gb, TN)
                later = qg if later is None else later + qg


def back_local(idx, cuts, scale, q, k, v, g, state, filled, half_heads, after):
    rows, width = q.shape
    block = math.gcd(rows, 256)
    heads = half_heads // cuts
    group = math.gcd(heads, 2)
    steps = heads // group
    wide = group * DH
    mine = pl.BlockSpec((rows, wide), lambda i, s: (0, (s[0] * cuts + s[1]) * steps + i))
    own = pl.BlockSpec((rows, wide), lambda i, s: (0, s[1] * steps + i))
    extra = len(filled)
    half = sds((rows, half_heads * DH), F32)
    return call(
        functools.partial(back_body, group, block, scale, extra),
        (steps,),
        [
            mine,
            mine,
            mine,
            own,
            pl.BlockSpec((group, DH, DH), lambda i, s: (s[1] * steps + i, 0, 0)),
        ]
        + [pl.BlockSpec(memory_space=pl.ANY)] * extra,
        [mine, own, own],
        [sds((rows, width), F32), half, half],
        2 * rows * DH * (5 * block + 4 * DH) * heads,
        rows * DH * heads * 20,
        {6 + n: n for n in range(extra)},
        after=after,
        vmem=58,
        token=True,
    )(idx, q, k, v, g, state, *filled)


def later_body(heads, scale, extra, idx, k, v, later, dk_in, dv_in, *refs):
    dk, dv = refs[extra:]
    for i in range(heads):
        c = cut(i)
        dk[:, c] = scale * (dk_in[:, c] + dot(v[:, c], later[i], NT))
        dv[:, c] = scale * (dv_in[:, c] + dot(k[:, c], later[i]))


def add_later(half, scale, k, v, later, dk, dv, filled, half_heads, after):
    rows, width = k.shape
    block = math.gcd(rows, 128)
    wide = half_heads * DH
    mine = pl.BlockSpec((block, wide), lambda i, s: (i, s[0]))
    own = pl.BlockSpec((block, wide), lambda i, s: (i, 0))
    extra = len(filled)
    return call(
        functools.partial(later_body, half_heads, scale, extra),
        (rows // block,),
        [mine, mine, pl.BlockSpec((half_heads, DH, DH), lambda i, s: (0, 0, 0)), own, own]
        + [pl.BlockSpec(memory_space=pl.ANY)] * extra,
        [mine, mine],
        [sds((rows, width), F32)] * 2,
        4 * rows * DH * DH * half_heads,
        rows * DH * half_heads * 20,
        {6 + n: n for n in range(extra)},
        after=after,
        vmem=58,
    )(half, k, v, later, dk, dv, *filled)


def tie(array, *others):
    return lax.optimization_barrier((array,) + others)


def swap(array, axis, bit):
    size = lax.axis_size(axis)
    return lax.ppermute(array, axis, [(i, i ^ (1 << bit)) for i in range(size)])


def scan_states(theirs, mine, ctx_bits, flipped, fill):
    pos = lax.axis_index("ctx")
    if flipped:
        pos = lax.axis_size("ctx") - 1 - pos

    held = []

    def beside(step, sent, got):
        done = fill[step]([sent, *held]) if step in fill else held
        got, *held[:] = tie(got, *done)
        return got.astype(F32)

    got = beside(0, theirs, swap(theirs, "ctx", 0))
    own = mine.astype(F32)
    total = own + got
    prefix = jnp.zeros_like(total)
    for bit in range(1, ctx_bits):
        sent = total.astype(BF16)
        other = beside(bit, sent, swap(sent, "ctx", bit))
        prefix = prefix + jnp.where((pos >> bit) & 1 == 1, other, 0.0)
        total = total + other
    upper = pos & 1 == 1
    mine_prefix = (prefix + jnp.where(upper, got, 0.0)).astype(BF16)
    sent = (prefix + jnp.where(upper, 0.0, own)).astype(BF16)
    return mine_prefix, swap(sent, "ctx", 0), held


def cuts_of(tiles, sizes):
    ends, at = [], 0
    for size in sizes:
        at = min(at + size, tiles)
        ends.append(at)
    ends[-1] = tiles
    starts = [0] + ends[:-1]
    return [(lo, hi) for lo, hi in zip(starts, ends) if lo < hi]


def on_device(queries, keys, values, teacher, out_weight, valid):
    rows, width = queries.shape
    heads = width // DH
    half_heads = heads // 2
    ctx_size = lax.axis_size("ctx")
    ctx_bits = ctx_size.bit_length() - 1
    chips = lax.axis_size("head") // 2
    ctx_id, head_id = lax.axis_index("ctx"), lax.axis_index("head")
    chip, core = head_id // 2, head_id % 2
    scale = 1.0 / math.sqrt(DH * rows * ctx_size)
    piece_width = teacher.shape[1]
    tile = 256 if piece_width % 256 == 0 else 128
    tiles = piece_width // tile
    sum_spans = [(lo * tile, hi * tile) for lo, hi in cuts_of(tiles, (2, 2, 1))]
    error_spans = [(lo * tile, hi * tile) for lo, hi in cuts_of(tiles, (2, 2, 1))]

    my_half = ctx_id & 1
    mine_ix = my_half[None].astype(jnp.int32)
    theirs_ix = 1 - mine_ix

    kv_theirs = kv_states(theirs_ix, keys, values, half_heads)
    kv_mine = kv_states(mine_ix, keys, values, half_heads, after=[kv_theirs])
    parts = {}

    def beside_forward(step):
        def run(after):
            if step == min(1, ctx_bits - 1):
                parts["mine"] = intra(mine_ix, queries, keys, values, half_heads, after)
                after = [parts["mine"]]
            if step == ctx_bits - 1:
                parts["theirs"] = intra(theirs_ix, queries, keys, values, half_heads, after)
                count, *after = tie(jnp.full((8, 128), jnp.sum(valid), jnp.int32), *after)
                token = parts["theirs"]
                for bit in range(ctx_bits - 1):
                    got, token = tie(swap(count, "ctx", bit), token)
                    count = count + got
                after = [token, count]
            return after if step else []

        return run

    before_mine, before_theirs, (*_, count) = scan_states(
        kv_theirs, kv_mine, ctx_bits, False, {n: beside_forward(n) for n in range(ctx_bits)}
    )
    count = count + swap(count, "ctx", ctx_bits - 1)
    before_theirs, count = tie(before_theirs, count)
    other_weight = swap(out_weight, "head", 0)

    def both_cores(array):
        return array, swap(array, "head", 0)

    attn_mine = both_cores(
        attend(mine_ix, scale, queries, parts["mine"], before_mine, half_heads)
    )
    attn_theirs = both_cores(
        attend(theirs_ix, scale, queries, parts["theirs"], before_theirs, half_heads)
    )

    def column(to_chip, to_core, lo):
        return ((to_chip * 2 + to_core) * piece_width + lo) // 128

    def terms(by, lo, hi, after=()):
        start = column(lax.rem(chip + by, chips), core, lo)
        idx = jnp.stack([my_half, 1 - my_half, start]).astype(jnp.int32)
        return project(idx, attn_mine, attn_theirs, out_weight, other_weight, hi - lo, after)

    def shift(array, by):
        size = 2 * chips
        return lax.ppermute(array, "head", [(i, (i + 2 * by) % size) for i in range(size)])

    arrived, own, after = [], [], []
    first = sum_spans[0][1]
    for n, (lo, hi) in enumerate(sum_spans):
        got = []
        if n == 2:
            own.append(terms(0, 0, first, after))
            after = [own[0], *arrived[0]]
        for by in range(1, chips):
            summed = terms(by, lo, hi, after)
            after = [summed]
            got.append(shift(summed, by))
        arrived.append(got)
    if own:
        own.append(terms(0, first, piece_width, after + arrived[1]))
    else:
        own.append(terms(0, 0, piece_width, after))
    own_spans = [(0, first), (first, piece_width)] if len(own) > 1 else [(0, piece_width)]

    factor = rows * ctx_size / count[0, 0].astype(F32)
    weigh = (valid.astype(F32) * factor)[:, None]

    def columns(pieces, spans, lo, hi):
        inside = [
            piece[:, max(lo - base, 0) : hi - base].astype(F32)
            for (base, end), piece in zip(spans, pieces)
            if base < hi and lo < end
        ]
        return jnp.concatenate(inside, 1)

    def error_of(lo, hi):
        predicted = columns(own, own_spans, lo, hi)
        for by in range(1, chips):
            predicted = predicted + columns([got[by - 1] for got in arrived], sum_spans, lo, hi)
        return (weigh * (predicted - teacher[:, lo:hi].astype(F32))).astype(BF16)

    errors = [error_of(lo, hi) for lo, hi in error_spans]
    near = [errors, [swap(error, "head", 0) for error in errors]]
    idx = jnp.stack([chip * 2 + core, chip * 2 + 1 - core]).astype(jnp.int32)
    acc, summed_near = grad_accumulate(
        idx, near, None, error_spans, out_weight, piece_width
    )

    early = max(1, len(error_spans) - 2)
    gathered = [[shift(error, by) for by in range(1, chips)] for error in errors]

    def sources(select, token):
        groups, devices = [], []
        for by in range(1, chips):
            from_chip = lax.rem(chip + chips - by, chips)
            pieces = [got[by - 1] for got in gathered[select]]
            *late, token = tie(pieces[0], *pieces[1:], token)
            groups += [pieces, [swap(piece, "head", 0) for piece in late]]
            devices += [(from_chip, core), (from_chip, 1 - core)]
        return groups, devices, token

    last, last_ix, token = [], [], summed_near
    if chips > 1:
        far, devices, token = sources(slice(0, early), summed_near)
        far_ix = jnp.stack([to_chip * 2 + to_core for to_chip, to_core in devices])
        acc, summed_far = grad_accumulate(
            far_ix.astype(jnp.int32), far, acc, error_spans[:early], out_weight, piece_width,
            [token],
        )
        last, devices, token = sources(slice(early, None), summed_far)
        last_ix = [column(*device, error_spans[early][0]) for device in devices]

    def last_of(ix, after=()):
        index = jnp.stack([ix[0]] + last_ix).astype(jnp.int32)
        return grad_last(index, acc, queries, last, out_weight, half_heads, after)

    g_theirs, r_theirs = last_of(theirs_ix, [token])
    g_mine, r_mine = last_of(mine_ix, [r_theirs])
    cuts = 1
    done_q, done_kv = [], {"theirs": [], "mine": []}
    halves = {
        "theirs": (theirs_ix[0], g_theirs, before_theirs),
        "mine": (mine_ix[0], g_mine, before_mine),
    }

    def back(name, part, after):
        half, g, before = halves[name]
        *got, token = back_local(
            jnp.stack([half, jnp.int32(part)]), cuts, scale, queries, keys, values, g, before,
            done_q + done_kv[name], half_heads, after,
        )
        done_q[:], done_kv[name] = got[:1], got[1:]
        return [token]

    order = [(name, part) for name in ("mine", "theirs") for part in range(cuts)]
    plan = {}
    for n, step in enumerate((1, 2)):
        if n < len(order):
            plan.setdefault(min(step, ctx_bits - 1), []).append(order[n])

    def beside_backward(step):
        def run(after):
            if step == 0:
                return [r_mine]
            for name, part in plan.get(step, []):
                after = back(name, part, after)
            return after

        return run

    later_mine, later_theirs, token = scan_states(
        r_theirs, r_mine, ctx_bits, True, {n: beside_backward(n) for n in range(ctx_bits)}
    )
    (q_grad,) = done_q
    grads = add_later(
        mine_ix, scale, keys, values, later_mine, *done_kv["mine"], [], half_heads, token
    )
    k_grad, v_grad = add_later(
        theirs_ix, scale, keys, values, later_theirs, *done_kv["theirs"], list(grads), half_heads, []
    )
    return q_grad, k_grad, v_grad


def solution(mesh):
    in_specs = (
        P("ctx", "head"),
        P("ctx", "head"),
        P("ctx", "head"),
        P("ctx", "head"),
        P("head", None),
        P("ctx"),
    )
    out_specs = (P("ctx", "head"), P("ctx", "head"), P("ctx", "head"))
    return jax.shard_map(
        on_device, mesh=mesh, in_specs=in_specs, out_specs=out_specs, check_vma=False
    )
```

```python
import functools
import math

import jax
import jax.numpy as jnp
from jax import lax
from jax.experimental import pallas as pl
from jax.experimental.pallas import tpu as pltpu
from jax.sharding import PartitionSpec as P

DH = 128
GROUP = 4
HINT = 1000000000000
NT = (((1,), (1,)), ((), ()))
TN = (((0,), (0,)), ((), ()))
F32 = jnp.float32
BF16 = jnp.bfloat16


def dot(a, b, dims=(((1,), (0,)), ((), ()))):
    return lax.dot_general(a, b, dims, preferred_element_type=F32)


def call(body, grid, in_specs, out_specs, out_shape, flops, moved, aliases=None, after=(), vmem=40, scratch=(), token=False):
    count = len(in_specs)
    if token:
        out_specs = [*out_specs, pl.BlockSpec((8, 128), lambda *_: (0, 0))]
        out_shape = [*out_shape, sds((8, 128), F32)]

    def ordered(idx, *refs):
        refs = list(refs)
        if token:
            refs.pop(count + len(after) + len(out_shape) - 1)[...] = jnp.zeros((8, 128), F32)
        body(idx, *refs[:count], *refs[count + len(after) :])

    kernel = pl.pallas_call(
        ordered,
        grid_spec=pltpu.PrefetchScalarGridSpec(
            num_scalar_prefetch=1,
            grid=grid,
            in_specs=list(in_specs) + [pl.BlockSpec(memory_space=pl.ANY)] * len(after),
            out_specs=out_specs,
            scratch_shapes=list(scratch),
        ),
        out_shape=out_shape,
        input_output_aliases=aliases or {},
        compiler_params=pltpu.CompilerParams(vmem_limit_bytes=vmem * 1024 * 1024),
        cost_estimate=pl.CostEstimate(
            flops=max(1, flops // HINT), bytes_accessed=max(1, moved // HINT), transcendentals=0
        ),
    )
    return lambda *args: kernel(*args, *after)


def sds(shape, dtype):
    return jax.ShapeDtypeStruct(shape, dtype)


def lower_mask(n):
    rows = lax.broadcasted_iota(jnp.int32, (n, n), 0)
    cols = lax.broadcasted_iota(jnp.int32, (n, n), 1)
    return rows >= cols


def cut(i):
    return slice(i * DH, (i + 1) * DH)


def group_of(half_heads):
    return math.gcd(half_heads, GROUP)


def kv_body(group, idx, k, v, out):
    for i in range(group):
        out[i] = dot(k[:, cut(i)], v[:, cut(i)], TN).astype(BF16)


def kv_states(half, k, v, half_heads, after=()):
    rows = k.shape[0]
    group = group_of(half_heads)
    steps = half_heads // group
    blk = pl.BlockSpec((rows, group * DH), lambda i, s: (0, s[0] * steps + i))
    return call(
        functools.partial(kv_body, group),
        (steps,),
        [blk, blk],
        pl.BlockSpec((group, DH, DH), lambda i, s: (i, 0, 0)),
        sds((half_heads, DH, DH), BF16),
        2 * rows * DH * DH * half_heads,
        rows * DH * half_heads * 4,
        after=after,
        vmem=58,
    )(half, k, v)


def intra_body(group, block, idx, q, k, v, out):
    mask = lower_mask(block)
    n = q.shape[0] // block
    for i in range(group):
        c = cut(i)
        state = None
        for b in range(n):
            r = slice(b * block, (b + 1) * block)
            qb, kb, vb = q[r, c], k[r, c], v[r, c]
            s = jnp.where(mask, dot(qb, kb, NT), 0.0).astype(BF16)
            o = dot(s, vb)
            if state is not None:
                o = o + dot(qb, state.astype(BF16))
            if b < n - 1:
                kv = dot(kb, vb, TN)
                state = kv if state is None else state + kv
            out[r, c] = o


def intra(half, q, k, v, half_heads, after):
    rows = k.shape[0]
    block = math.gcd(rows, 256)
    group = group_of(half_heads)
    steps = half_heads // group
    blk = pl.BlockSpec((rows, group * DH), lambda i, s: (0, s[0] * steps + i))
    return call(
        functools.partial(intra_body, group, block),
        (steps,),
        [blk, blk, blk],
        pl.BlockSpec((rows, group * DH), lambda i, s: (0, i)),
        sds((rows, half_heads * DH), F32),
        4 * rows * (block + DH) * DH * half_heads,
        rows * DH * half_heads * 10,
        after=after,
        vmem=58,
    )(half, q, k, v)


def attn_body(group, scale, idx, q, part, state, out):
    for i in range(group):
        c = cut(i)
        out[:, c] = (scale * (part[:, c] + dot(q[:, c], state[i]))).astype(BF16)


def attend(half, scale, q, part, state, half_heads):
    rows = q.shape[0]
    group = group_of(half_heads)
    steps = half_heads // group
    blk = pl.BlockSpec((rows, group * DH), lambda i, s: (0, i))
    return call(
        functools.partial(attn_body, group, scale),
        (steps,),
        [
            pl.BlockSpec((rows, group * DH), lambda i, s: (0, s[0] * steps + i)),
            blk,
            pl.BlockSpec((group, DH, DH), lambda i, s: (i, 0, 0)),
        ],
        blk,
        sds((rows, half_heads * DH), BF16),
        2 * rows * DH * DH * half_heads,
        rows * DH * half_heads * 8,
    )(half, q, part, state)


def project_body(idx, a0, b0, a1, b1, w, wo, out, acc):
    i = pl.program_id(0)

    @pl.when(i == 0)
    def _():
        acc[...] = dot(a0[...], w[...]) + dot(b0[...], wo[...])

    @pl.when(i == 1)
    def _():
        out[...] = (acc[...] + dot(a1[...], w[...]) + dot(b1[...], wo[...])).astype(BF16)


def project(idx, mine, theirs, weight, other_weight, span, after=()):
    rows, depth = mine[0].shape
    whole = pl.BlockSpec((rows, depth), lambda i, s: (0, 0))
    return call(
        project_body,
        (2,),
        [
            whole,
            whole,
            whole,
            whole,
            pl.BlockSpec(
                (pl.Element(depth), pl.Element(span)), lambda i, s: (s[i] * depth, s[2] * 128)
            ),
            pl.BlockSpec(
                (pl.Element(depth), pl.Element(span)), lambda i, s: (s[i] * depth, s[2] * 128)
            ),
        ],
        pl.BlockSpec((rows, span), lambda i, s: (0, 0)),
        sds((rows, span), BF16),
        8 * rows * depth * span,
        8 * depth * span + 8 * rows * depth + 2 * rows * span,
        after=after,
        vmem=44,
        scratch=[pltpu.VMEM((rows, span), F32)],
    )(idx, *mine, *theirs, weight, other_weight)


def grad_body(counts, row_tile, with_acc, idx, *refs):
    refs = list(refs)
    cols = pl.ds(pl.multiple_of(pl.program_id(0) * row_tile, row_tile), row_tile)
    acc = refs.pop(0)[:, cols] if with_acc else None
    out = refs.pop()
    for count in counts:
        w, lo = refs[count], 0
        for piece in refs[:count]:
            hi = lo + piece.shape[1]
            t = dot(piece[...], w[:, lo:hi], NT)
            acc = t if acc is None else acc + t
            lo = hi
        refs = refs[count + 1 :]
    out[:, cols] = acc


def grad_accumulate(idx, groups, acc, weight, after=()):
    depth = weight.shape[0]
    rows = groups[0][0].shape[0]
    row_tile = math.gcd(depth, 512)
    vmem = pl.BlockSpec(memory_space=pltpu.VMEM)
    in_specs, args = [], []
    if acc is not None:
        in_specs.append(vmem)
        args.append(acc)
    total = 0
    for g, pieces in enumerate(groups):
        span = sum(piece.shape[1] for piece in pieces)
        total += span
        in_specs += [pl.BlockSpec(piece.shape, lambda i, s: (0, 0)) for piece in pieces]
        in_specs.append(
            pl.BlockSpec(
                (pl.Element(row_tile), pl.Element(span)),
                lambda i, s, g=g: (i * row_tile, s[g] * 128),
            )
        )
        args += [*pieces, weight]
    return call(
        functools.partial(
            grad_body, [len(pieces) for pieces in groups], row_tile, acc is not None
        ),
        (depth // row_tile,),
        in_specs,
        [vmem],
        [pltpu.VMEM((rows, depth), F32)],
        2 * rows * depth * total,
        2 * depth * total + 8 * rows * depth,
        None,
        after=after,
        vmem=44,
        token=True,
    )(idx, *args)


def last_body(group, counts, idx, acc, q, *refs):
    *refs, g_out, r_out = refs
    t = acc[...]
    for count in counts:
        w, lo = refs[count], 0
        for piece in refs[:count]:
            hi = lo + piece.shape[1]
            t = t + dot(piece[...], w[:, lo:hi], NT)
            lo = hi
        refs = refs[count + 1 :]
    g = t.astype(BF16)
    g_out[...] = g
    for i in range(group):
        r_out[i] = dot(q[:, cut(i)], g[:, cut(i)], TN).astype(BF16)


def grad_last(idx, acc, q, groups, weight, half_heads, after=()):
    rows = acc.shape[0]
    group = group_of(half_heads)
    steps = half_heads // group
    wide = group * DH
    mine = pl.BlockSpec((rows, wide), lambda i, s: (0, s[0] * steps + i))
    in_specs, args, total = [mine, mine], [acc, q], 0
    for n, pieces in enumerate(groups):
        span = sum(piece.shape[1] for piece in pieces)
        total += span
        in_specs += [pl.BlockSpec(piece.shape, lambda i, s: (0, 0)) for piece in pieces]
        in_specs.append(
            pl.BlockSpec(
                (pl.Element(wide), pl.Element(span)),
                lambda i, s, n=n: ((s[0] * steps + i) * wide, s[1 + n] * 128),
            )
        )
        args += pieces + [weight]
    return call(
        functools.partial(last_body, group, [len(pieces) for pieces in groups]),
        (steps,),
        in_specs,
        [
            pl.BlockSpec((rows, wide), lambda i, s: (0, i)),
            pl.BlockSpec((group, DH, DH), lambda i, s: (i, 0, 0)),
        ],
        [pltpu.HBM((rows, half_heads * DH), BF16), sds((half_heads, DH, DH), BF16)],
        2 * rows * half_heads * DH * (total + DH),
        half_heads * DH * (rows * 8 + 2 * total),
        after=after,
        vmem=44,
    )(idx, *args)


def back_body(group, block, scale, extra, idx, q, k, v, g, state, *refs):
    dq, dk, dv = refs[extra:]
    mask = lower_mask(block)
    n = q.shape[0] // block
    for i in range(group):
        c = cut(i)
        before = state[i].astype(F32)
        later = None
        dks, dvs = [], []
        for b in range(n):
            r = slice(b * block, (b + 1) * block)
            qb, kb, vb, gb = q[r, c], k[r, c], v[r, c], g[r, c]
            gs = jnp.where(mask, dot(gb, vb, NT), 0.0).astype(BF16)
            s = jnp.where(mask, dot(qb, kb, NT), 0.0).astype(BF16)
            dq[r, c] = scale * (dot(gs, kb) + dot(gb, before.astype(BF16), NT))
            dks.append(dot(gs, qb, TN))
            dvs.append(dot(s, gb, TN))
            if b < n - 1:
                before = before + dot(kb, vb, TN)
        for b in reversed(range(n)):
            r = slice(b * block, (b + 1) * block)
            qb, kb, vb, gb = q[r, c], k[r, c], v[r, c], g[r, c]
            dkb, dvb = dks[b], dvs[b]
            if later is not None:
                lb = later.astype(BF16)
                dkb = dkb + dot(vb, lb, NT)
                dvb = dvb + dot(kb, lb)
            dk[r, c] = dkb
            dv[r, c] = dvb
            if b > 0:
                qg = dot(qb, gb, TN)
                later = qg if later is None else later + qg


def back_local(idx, cuts, scale, q, k, v, g, state, filled, half_heads, after):
    rows, width = q.shape
    block = math.gcd(rows, 256)
    heads = half_heads // cuts
    group = math.gcd(heads, 2)
    steps = heads // group
    wide = group * DH
    mine = pl.BlockSpec((rows, wide), lambda i, s: (0, (s[0] * cuts + s[1]) * steps + i))
    own = pl.BlockSpec((rows, wide), lambda i, s: (0, s[1] * steps + i))
    extra = len(filled)
    half = sds((rows, half_heads * DH), F32)
    return call(
        functools.partial(back_body, group, block, scale, extra),
        (steps,),
        [
            mine,
            mine,
            mine,
            own,
            pl.BlockSpec((group, DH, DH), lambda i, s: (s[1] * steps + i, 0, 0)),
        ]
        + [pl.BlockSpec(memory_space=pl.ANY)] * extra,
        [mine, own, own],
        [sds((rows, width), F32), half, half],
        2 * rows * DH * (5 * block + 4 * DH) * heads,
        rows * DH * heads * 20,
        {6 + n: n for n in range(extra)},
        after=after,
        vmem=58,
        token=True,
    )(idx, q, k, v, g, state, *filled)


def later_body(heads, scale, extra, idx, k, v, later, dk_in, dv_in, *refs):
    dk, dv = refs[extra:]
    for i in range(heads):
        c = cut(i)
        dk[:, c] = scale * (dk_in[:, c] + dot(v[:, c], later[i], NT))
        dv[:, c] = scale * (dv_in[:, c] + dot(k[:, c], later[i]))


def add_later(half, scale, k, v, later, dk, dv, filled, half_heads, after):
    rows, width = k.shape
    block = math.gcd(rows, 128)
    wide = half_heads * DH
    mine = pl.BlockSpec((block, wide), lambda i, s: (i, s[0]))
    own = pl.BlockSpec((block, wide), lambda i, s: (i, 0))
    extra = len(filled)
    return call(
        functools.partial(later_body, half_heads, scale, extra),
        (rows // block,),
        [mine, mine, pl.BlockSpec((half_heads, DH, DH), lambda i, s: (0, 0, 0)), own, own]
        + [pl.BlockSpec(memory_space=pl.ANY)] * extra,
        [mine, mine],
        [sds((rows, width), F32)] * 2,
        4 * rows * DH * DH * half_heads,
        rows * DH * half_heads * 20,
        {6 + n: n for n in range(extra)},
        after=after,
        vmem=24,
    )(half, k, v, later, dk, dv, *filled)


def tie(array, *others):
    return lax.optimization_barrier((array,) + others)


def swap(array, axis, bit):
    size = lax.axis_size(axis)
    return lax.ppermute(array, axis, [(i, i ^ (1 << bit)) for i in range(size)])


def scan_states(theirs, mine, ctx_bits, flipped, fill):
    pos = lax.axis_index("ctx")
    if flipped:
        pos = lax.axis_size("ctx") - 1 - pos

    held = []

    def beside(step, sent, got):
        done = fill[step]([sent, *held]) if step in fill else held
        got, *held[:] = tie(got, *done)
        return got.astype(F32)

    got = beside(0, theirs, swap(theirs, "ctx", 0))
    own = mine.astype(F32)
    total = own + got
    prefix = jnp.zeros_like(total)
    for bit in range(1, ctx_bits):
        sent = total.astype(BF16)
        other = beside(bit, sent, swap(sent, "ctx", bit))
        prefix = prefix + jnp.where((pos >> bit) & 1 == 1, other, 0.0)
        total = total + other
    upper = pos & 1 == 1
    mine_prefix = (prefix + jnp.where(upper, got, 0.0)).astype(BF16)
    sent = (prefix + jnp.where(upper, 0.0, own)).astype(BF16)
    return mine_prefix, swap(sent, "ctx", 0), held


def cuts_of(tiles, sizes):
    ends, at = [], 0
    for size in sizes:
        at = min(at + size, tiles)
        ends.append(at)
    ends[-1] = tiles
    starts = [0] + ends[:-1]
    return [(lo, hi) for lo, hi in zip(starts, ends) if lo < hi]


def on_device(queries, keys, values, teacher, out_weight, valid):
    rows, width = queries.shape
    heads = width // DH
    half_heads = heads // 2
    ctx_size = lax.axis_size("ctx")
    ctx_bits = ctx_size.bit_length() - 1
    chips = lax.axis_size("head") // 2
    ctx_id, head_id = lax.axis_index("ctx"), lax.axis_index("head")
    chip, core = head_id // 2, head_id % 2
    scale = 1.0 / math.sqrt(DH * rows * ctx_size)
    piece_width = teacher.shape[1]
    tile = 256 if piece_width % 256 == 0 else 128
    tiles = piece_width // tile
    sum_spans = [(lo * tile, hi * tile) for lo, hi in cuts_of(tiles, (2, 2, 1))]
    error_spans = [(lo * tile, hi * tile) for lo, hi in cuts_of(tiles, (3, 2))]

    my_half = ctx_id & 1
    mine_ix = my_half[None].astype(jnp.int32)
    theirs_ix = 1 - mine_ix

    kv_theirs = kv_states(theirs_ix, keys, values, half_heads)
    kv_mine = kv_states(mine_ix, keys, values, half_heads, after=[kv_theirs])
    parts = {}

    def beside_forward(step):
        def run(after):
            if step == min(1, ctx_bits - 1):
                parts["mine"] = intra(mine_ix, queries, keys, values, half_heads, after)
                after = [parts["mine"]]
            if step == ctx_bits - 1:
                parts["theirs"] = intra(theirs_ix, queries, keys, values, half_heads, after)
                count, *after = tie(jnp.full((8, 128), jnp.sum(valid), jnp.int32), *after)
                token = parts["theirs"]
                for bit in range(ctx_bits - 1):
                    got, token = tie(swap(count, "ctx", bit), token)
                    count = count + got
                after = [token, count]
            return after if step else []

        return run

    before_mine, before_theirs, (*_, count) = scan_states(
        kv_theirs, kv_mine, ctx_bits, False, {n: beside_forward(n) for n in range(ctx_bits)}
    )
    count = count + swap(count, "ctx", ctx_bits - 1)
    before_theirs, count = tie(before_theirs, count)
    other_weight = swap(out_weight, "head", 0)

    def both_cores(array):
        return array, swap(array, "head", 0)

    attn_mine = both_cores(
        attend(mine_ix, scale, queries, parts["mine"], before_mine, half_heads)
    )
    attn_theirs = both_cores(
        attend(theirs_ix, scale, queries, parts["theirs"], before_theirs, half_heads)
    )

    def column(to_chip, to_core, lo):
        return ((to_chip * 2 + to_core) * piece_width + lo) // 128

    def terms(by, lo, hi, after=()):
        start = column(lax.rem(chip + by, chips), core, lo)
        idx = jnp.stack([my_half, 1 - my_half, start]).astype(jnp.int32)
        return project(idx, attn_mine, attn_theirs, out_weight, other_weight, hi - lo, after)

    def shift(array, by):
        size = 2 * chips
        return lax.ppermute(array, "head", [(i, (i + 2 * by) % size) for i in range(size)])

    arrived, own, after = [], [], []
    first = sum_spans[0][1]
    for n, (lo, hi) in enumerate(sum_spans):
        got = []
        if n == 1:
            own.append(terms(0, 0, first, after))
            after = [own[0]]
        if n == 2:
            after = after + arrived[0]
        for by in range(1, chips):
            summed = terms(by, lo, hi, after)
            after = [summed]
            got.append(shift(summed, by))
        arrived.append(got)
    if first < piece_width:
        own.append(terms(0, first, piece_width, after))
    else:
        own.append(terms(0, 0, piece_width, after))
    own_spans = [(0, first), (first, piece_width)] if len(own) > 1 else [(0, piece_width)]

    factor = rows * ctx_size / count[0, 0].astype(F32)
    weigh = (valid.astype(F32) * factor)[:, None]

    def columns(pieces, spans, lo, hi):
        inside = [
            piece[:, max(lo - base, 0) : hi - base].astype(F32)
            for (base, end), piece in zip(spans, pieces)
            if base < hi and lo < end
        ]
        return jnp.concatenate(inside, 1)

    def error_of(lo, hi):
        predicted = columns(own, own_spans, lo, hi)
        for by in range(1, chips):
            predicted = predicted + columns([got[by - 1] for got in arrived], sum_spans, lo, hi)
        return (weigh * (predicted - teacher[:, lo:hi].astype(F32))).astype(BF16)

    errors = [error_of(lo, hi) for lo, hi in error_spans]
    near = [errors, [swap(error, "head", 0) for error in errors]]
    idx = jnp.stack([column(chip, core, 0), column(chip, 1 - core, 0)]).astype(jnp.int32)
    acc, summed_near = grad_accumulate(idx, near, None, out_weight)

    early = max(1, len(error_spans) - 1)
    gathered = [[shift(error, by) for by in range(1, chips)] for error in errors]

    def sources(select, token):
        groups, devices = [], []
        for by in range(1, chips):
            from_chip = lax.rem(chip + chips - by, chips)
            pieces = [got[by - 1] for got in gathered[select]]
            *late, token = tie(pieces[0], *pieces[1:], token)
            groups += [pieces, [swap(piece, "head", 0) for piece in late]]
            devices += [(from_chip, core), (from_chip, 1 - core)]
        return groups, devices, token

    last, last_ix, token = [], [], summed_near
    if chips > 1:
        far, devices, token = sources(slice(0, early), summed_near)
        far_ix = jnp.stack([column(*device, 0) for device in devices]).astype(jnp.int32)
        acc, summed_far = grad_accumulate(far_ix, far, acc, out_weight, [token])
        last, devices, token = sources(slice(early, None), summed_far)
        last_ix = [column(*device, error_spans[early][0]) for device in devices]

    def last_of(ix, after=()):
        index = jnp.stack([ix[0]] + last_ix).astype(jnp.int32)
        return grad_last(index, acc, queries, last, out_weight, half_heads, after)

    g_theirs, r_theirs = last_of(theirs_ix, [token])
    g_mine, r_mine = last_of(mine_ix, [r_theirs])
    cuts = 1
    done_q, done_kv = [], {"theirs": [], "mine": []}
    halves = {
        "theirs": (theirs_ix[0], g_theirs, before_theirs),
        "mine": (mine_ix[0], g_mine, before_mine),
    }

    def back(name, part, after):
        half, g, before = halves[name]
        *got, token = back_local(
            jnp.stack([half, jnp.int32(part)]), cuts, scale, queries, keys, values, g, before,
            done_q + done_kv[name], half_heads, after,
        )
        done_q[:], done_kv[name] = got[:1], got[1:]
        return [token]

    order = [(name, part) for name in ("mine", "theirs") for part in range(cuts)]
    plan = {}
    for n, step in enumerate((1, 2)):
        if n < len(order):
            plan.setdefault(min(step, ctx_bits - 1), []).append(order[n])

    def beside_backward(step):
        def run(after):
            if step == 0:
                return [r_mine]
            for name, part in plan.get(step, []):
                after = back(name, part, after)
            return after

        return run

    later_mine, later_theirs, token = scan_states(
        r_theirs, r_mine, ctx_bits, True, {n: beside_backward(n) for n in range(ctx_bits)}
    )
    (q_grad,) = done_q
    grads = add_later(
        mine_ix, scale, keys, values, later_mine, *done_kv["mine"], [], half_heads, token
    )
    k_grad, v_grad = add_later(
        theirs_ix, scale, keys, values, later_theirs, *done_kv["theirs"], list(grads), half_heads, []
    )
    return q_grad, k_grad, v_grad


def solution(mesh):
    in_specs = (
        P("ctx", "head"),
        P("ctx", "head"),
        P("ctx", "head"),
        P("ctx", "head"),
        P("head", None),
        P("ctx"),
    )
    out_specs = (P("ctx", "head"), P("ctx", "head"), P("ctx", "head"))
    return jax.shard_map(
        on_device, mesh=mesh, in_specs=in_specs, out_specs=out_specs, check_vma=False
    )
```

```python
import functools
import math

import jax
import jax.numpy as jnp
from jax import lax
from jax.experimental import pallas as pl
from jax.experimental.pallas import tpu as pltpu
from jax.sharding import PartitionSpec as P

DH = 128
GROUP = 4
HINT = 1000000000000
NT = (((1,), (1,)), ((), ()))
TN = (((0,), (0,)), ((), ()))
F32 = jnp.float32
BF16 = jnp.bfloat16


def dot(a, b, dims=(((1,), (0,)), ((), ()))):
    return lax.dot_general(a, b, dims, preferred_element_type=F32)


class Entries:
    def __init__(self, refs, at):
        self.refs, self.at = refs, at

    def __getitem__(self, n):
        if not isinstance(n, int):
            return jnp.where(n == 0, self[0], self[1])
        more = self.at[n][1]
        return self.refs[n][0] + more if more else self.refs[n][0]


def call(body, at, grid, in_specs, out_specs, out_shape, flops, moved, aliases=None, after=(), vmem=40, scratch=(), token=False):
    count = len(in_specs)
    many = isinstance(out_specs, (list, tuple))
    if token:
        out_specs = [*out_specs, pl.BlockSpec((8, 128), lambda i, s: (0, 0))]
        out_shape = [*out_shape, sds((8, 128), F32)]

    def seen(spec):
        if spec.index_map is None:
            return spec
        index_map = spec.index_map
        return pl.BlockSpec(spec.block_shape, lambda i, *s: index_map(i, Entries(s, at)))

    in_specs = [seen(spec) for spec in in_specs]
    out_specs = [seen(spec) for spec in out_specs] if many else seen(out_specs)

    def ordered(*refs):
        scalars, refs = refs[: len(at)], list(refs[len(at) :])
        if token:
            refs.pop(count + len(after) + len(out_shape) - 1)[...] = jnp.zeros((8, 128), F32)
        body(Entries(scalars, at), *refs[:count], *refs[count + len(after) :])

    kernel = pl.pallas_call(
        ordered,
        grid_spec=pltpu.PrefetchScalarGridSpec(
            num_scalar_prefetch=len(at),
            grid=grid,
            in_specs=list(in_specs) + [pl.BlockSpec(memory_space=pl.ANY)] * len(after),
            out_specs=out_specs,
            scratch_shapes=list(scratch),
        ),
        out_shape=out_shape,
        input_output_aliases={n + len(at) - 1: m for n, m in (aliases or {}).items()},
        compiler_params=pltpu.CompilerParams(vmem_limit_bytes=vmem * 1024 * 1024),
        cost_estimate=pl.CostEstimate(
            flops=max(1, flops // HINT), bytes_accessed=max(1, moved // HINT), transcendentals=0
        ),
    )
    return lambda table, *args: kernel(*(table[n] for n, _ in at), *args, *after)


def sds(shape, dtype):
    return jax.ShapeDtypeStruct(shape, dtype)


def lower_mask(n):
    rows = lax.broadcasted_iota(jnp.int32, (n, n), 0)
    cols = lax.broadcasted_iota(jnp.int32, (n, n), 1)
    return rows >= cols


def cut(i):
    return slice(i * DH, (i + 1) * DH)


def group_of(half_heads):
    return math.gcd(half_heads, GROUP)


def kv_body(group, chunks, idx, k, v, *outs):
    for n, out in enumerate(outs):

        @pl.when(pl.program_id(0) == n)
        def _(out=out):
            for i in range(group):
                out[i] = dot(k[:, cut(i)], v[:, cut(i)], TN).astype(BF16)


def kv_states(table, at, k, v, heads, chunks, after=()):
    rows = k.shape[0]
    blk = pl.BlockSpec((rows, heads * DH), lambda i, s: (0, s[0] * chunks + i))
    return call(
        functools.partial(kv_body, heads, chunks),
        at,
        (chunks,),
        [blk, blk],
        [pl.BlockSpec((heads, DH, DH), lambda i, s: (0, 0, 0))] * chunks,
        [sds((heads, DH, DH), BF16)] * chunks,
        2 * rows * DH * DH * heads * chunks,
        rows * DH * heads * chunks * 4,
        after=after,
        vmem=58,
    )(table, k, v)


def intra_body(group, block, idx, q, k, v, out):
    mask = lower_mask(block)
    n = q.shape[0] // block
    for i in range(group):
        c = cut(i)
        state = None
        for b in range(n):
            r = slice(b * block, (b + 1) * block)
            qb, kb, vb = q[r, c], k[r, c], v[r, c]
            s = jnp.where(mask, dot(qb, kb, NT), 0.0).astype(BF16)
            o = dot(s, vb)
            if state is not None:
                o = o + dot(qb, state.astype(BF16))
            if b < n - 1:
                kv = dot(kb, vb, TN)
                state = kv if state is None else state + kv
            out[r, c] = o


def intra(table, at, q, k, v, half_heads, after):
    rows = k.shape[0]
    block = math.gcd(rows, 256)
    group = group_of(half_heads)
    steps = half_heads // group
    blk = pl.BlockSpec((rows, group * DH), lambda i, s: (0, s[0] * steps + i))
    return call(
        functools.partial(intra_body, group, block),
        at,
        (steps,),
        [blk, blk, blk],
        pl.BlockSpec((rows, group * DH), lambda i, s: (0, i)),
        sds((rows, half_heads * DH), F32),
        4 * rows * (block + DH) * DH * half_heads,
        rows * DH * half_heads * 10,
        after=after,
        vmem=58,
    )(table, q, k, v)


def attn_body(heads, scale, idx, q, part, *refs):
    *states, out = refs
    for n, state in enumerate(states):

        @pl.when(pl.program_id(0) == n)
        def _(state=state):
            for i in range(heads):
                c = cut(i)
                out[:, c] = (scale * (part[:, c] + dot(q[:, c], state[i]))).astype(BF16)


def attend(table, at, scale, q, part, states):
    rows = q.shape[0]
    chunks, heads = len(states), states[0].shape[0]
    blk = pl.BlockSpec((rows, heads * DH), lambda i, s: (0, i))
    return call(
        functools.partial(attn_body, heads, scale),
        at,
        (chunks,),
        [
            pl.BlockSpec((rows, heads * DH), lambda i, s: (0, s[0] * chunks + i)),
            blk,
        ]
        + [pl.BlockSpec((heads, DH, DH), lambda i, s: (0, 0, 0))] * chunks,
        blk,
        sds((rows, chunks * heads * DH), BF16),
        2 * rows * DH * DH * heads * chunks,
        rows * DH * heads * chunks * 8,
    )(table, q, part, *states)


def project_body(idx, a0, b0, a1, b1, w, wo, out, acc):
    i = pl.program_id(0)

    @pl.when(i == 0)
    def _():
        acc[...] = dot(a0[...], w[...]) + dot(b0[...], wo[...])

    @pl.when(i == 1)
    def _():
        out[...] = (acc[...] + dot(a1[...], w[...]) + dot(b1[...], wo[...])).astype(BF16)


def project(table, at, mine, theirs, weight, other_weight, span, after=()):
    rows, depth = mine[0].shape
    whole = pl.BlockSpec((rows, depth), lambda i, s: (0, 0))
    return call(
        project_body,
        at,
        (2,),
        [
            whole,
            whole,
            whole,
            whole,
            pl.BlockSpec(
                (pl.Element(depth), pl.Element(span)), lambda i, s: (s[i] * depth, s[2] * 128)
            ),
            pl.BlockSpec(
                (pl.Element(depth), pl.Element(span)), lambda i, s: (s[i] * depth, s[2] * 128)
            ),
        ],
        pl.BlockSpec((rows, span), lambda i, s: (0, 0)),
        sds((rows, span), BF16),
        8 * rows * depth * span,
        8 * depth * span + 8 * rows * depth + 2 * rows * span,
        after=after,
        vmem=44,
        scratch=[pltpu.VMEM((rows, span), F32)],
    )(table, *mine, *theirs, weight, other_weight)


def grad_body(counts, with_acc, idx, *refs):
    refs = list(refs)
    acc = refs.pop(0)[...] if with_acc else None
    out = refs.pop()
    for count in counts:
        w, lo = refs[count], 0
        for piece in refs[:count]:
            hi = lo + piece.shape[1]
            t = dot(piece[...], w[:, lo:hi], NT)
            acc = t if acc is None else acc + t
            lo = hi
        refs = refs[count + 1 :]
    out[...] = acc


def grad_accumulate(table, at, groups, acc, weight, after=()):
    depth = weight.shape[0]
    rows = groups[0][0].shape[0]
    row_tile = math.gcd(depth, 512)
    in_specs, args = [], []
    if acc is not None:
        in_specs.append(pl.BlockSpec((rows, row_tile), lambda i, s: (0, i)))
        args.append(pltpu.with_memory_space_constraint(acc, pltpu.HBM))
    total = 0
    for g, pieces in enumerate(groups):
        span = sum(piece.shape[1] for piece in pieces)
        total += span
        in_specs += [pl.BlockSpec(piece.shape, lambda i, s: (0, 0)) for piece in pieces]
        in_specs.append(
            pl.BlockSpec(
                (pl.Element(row_tile), pl.Element(span)),
                lambda i, s, g=g: (i * row_tile, s[g] * 128),
            )
        )
        args += [*pieces, weight]
    return call(
        functools.partial(grad_body, [len(pieces) for pieces in groups], acc is not None),
        at,
        (depth // row_tile,),
        in_specs,
        [pl.BlockSpec((rows, row_tile), lambda i, s: (0, i))],
        [pltpu.HBM((rows, depth), F32)],
        2 * rows * depth * total,
        2 * depth * total + 8 * rows * depth,
        None,
        after=after,
        vmem=44,
        token=True,
    )(table, *args)


def last_body(group, counts, idx, acc, q, *refs):
    *refs, g_out, r_out, held, sems = refs
    i = pl.program_id(0)
    wide = held.shape[2]
    steps = held.shape[0]

    def fetch(n):
        start = pl.multiple_of((idx[0] * steps + n) * wide, wide)
        return pltpu.make_async_copy(acc.at[:, pl.ds(start, wide)], held.at[n], sems.at[n])

    @pl.when(i == 0)
    def _():
        for n in range(steps):
            fetch(n).start()

    t = None
    for count in counts:
        w, lo = refs[count], 0
        for piece in refs[:count]:
            hi = lo + piece.shape[1]
            u = dot(piece[...], w[:, lo:hi], NT)
            t = u if t is None else t + u
            lo = hi
        refs = refs[count + 1 :]
    fetch(i).wait()
    t = held[i] if t is None else t + held[i]
    g = t.astype(BF16)
    g_out[...] = g
    for i in range(group):
        r_out[i] = dot(q[:, cut(i)], g[:, cut(i)], TN).astype(BF16)


def grad_last(table, at, acc, q, groups, weight, half_heads, after=()):
    rows = acc.shape[0]
    group = group_of(half_heads)
    steps = half_heads // group
    wide = group * DH
    mine = pl.BlockSpec((rows, wide), lambda i, s: (0, s[0] * steps + i))
    in_specs, total = [pl.BlockSpec(memory_space=pltpu.HBM), mine], 0
    args = [pltpu.with_memory_space_constraint(acc, pltpu.HBM), q]
    for n, pieces in enumerate(groups):
        span = sum(piece.shape[1] for piece in pieces)
        total += span
        in_specs += [pl.BlockSpec(piece.shape, lambda i, s: (0, 0)) for piece in pieces]
        in_specs.append(
            pl.BlockSpec(
                (pl.Element(wide), pl.Element(span)),
                lambda i, s, n=n: ((s[0] * steps + i) * wide, s[1 + n] * 128),
            )
        )
        args += [*pieces, weight]
    return call(
        functools.partial(last_body, group, [len(pieces) for pieces in groups]),
        at,
        (steps,),
        in_specs,
        [
            pl.BlockSpec((rows, wide), lambda i, s: (0, i)),
            pl.BlockSpec((group, DH, DH), lambda i, s: (i, 0, 0)),
        ],
        [pltpu.HBM((rows, half_heads * DH), BF16), sds((half_heads, DH, DH), BF16)],
        2 * rows * half_heads * DH * (total + DH),
        half_heads * DH * (rows * 8 + 2 * total),
        after=after,
        vmem=44,
        scratch=[
            pltpu.VMEM((steps, rows, wide), F32),
            pltpu.SemaphoreType.DMA((steps,)),
        ],
    )(table, *args)


def back_body(group, block, scale, extra, idx, q, k, v, g, state, *refs):
    dq, dk, dv = refs[extra:]
    mask = lower_mask(block)
    n = q.shape[0] // block
    for i in range(group):
        c = cut(i)
        before = state[i].astype(F32)
        later = None
        dks, dvs = [], []
        for b in range(n):
            r = slice(b * block, (b + 1) * block)
            qb, kb, vb, gb = q[r, c], k[r, c], v[r, c], g[r, c]
            gs = jnp.where(mask, dot(gb, vb, NT), 0.0).astype(BF16)
            s = jnp.where(mask, dot(qb, kb, NT), 0.0).astype(BF16)
            dq[r, c] = scale * (dot(gs, kb) + dot(gb, before.astype(BF16), NT))
            dks.append(dot(gs, qb, TN))
            dvs.append(dot(s, gb, TN))
            if b < n - 1:
                before = before + dot(kb, vb, TN)
        for b in reversed(range(n)):
            r = slice(b * block, (b + 1) * block)
            qb, kb, vb, gb = q[r, c], k[r, c], v[r, c], g[r, c]
            dkb, dvb = dks[b], dvs[b]
            if later is not None:
                lb = later.astype(BF16)
                dkb = dkb + dot(vb, lb, NT)
                dvb = dvb + dot(kb, lb)
            dk[r, c] = dkb.astype(dk.dtype)
            dv[r, c] = dvb.astype(dv.dtype)
            if b > 0:
                qg = dot(qb, gb, TN)
                later = qg if later is None else later + qg


def back_local(table, at, pairs, scale, q, k, v, g, state, filled, half_heads, after):
    rows, width = q.shape
    block = math.gcd(rows, 256)
    group = math.gcd(half_heads, 2)
    first, steps = pairs[0], pairs[1] - pairs[0]
    heads = group * steps
    wide = group * DH
    mine = pl.BlockSpec((rows, wide), lambda i, s: (0, s[0] * (half_heads // group) + first + i))
    own = pl.BlockSpec((rows, wide), lambda i, s: (0, first + i))
    extra = len(filled)
    half = sds((rows, half_heads * DH), BF16)
    return call(
        functools.partial(back_body, group, block, scale, extra),
        at,
        (steps,),
        [
            mine,
            mine,
            mine,
            own,
            pl.BlockSpec((group, DH, DH), lambda i, s: (first + i, 0, 0)),
        ]
        + [pl.BlockSpec(memory_space=pl.ANY)] * extra,
        [mine, own, own],
        [sds((rows, width), F32), half, half],
        2 * rows * DH * (5 * block + 4 * DH) * heads,
        rows * DH * heads * 20,
        {6 + n: n for n in range(extra)},
        after=after,
        vmem=58,
        token=True,
    )(table, q, k, v, g, state, *filled)


def later_body(heads, scale, extra, idx, k, v, later, dk_in, dv_in, *refs):
    dk, dv = refs[extra:]
    for i in range(heads):
        c = cut(i)
        dk[:, c] = scale * (dk_in[:, c] + dot(v[:, c], later[i], NT))
        dv[:, c] = scale * (dv_in[:, c] + dot(k[:, c], later[i]))


def add_later(table, at, scale, k, v, later, dk, dv, filled, half_heads, after):
    rows, width = k.shape
    block = math.gcd(rows, 128)
    wide = half_heads * DH
    mine = pl.BlockSpec((block, wide), lambda i, s: (i, s[0]))
    own = pl.BlockSpec((block, wide), lambda i, s: (i, 0))
    extra = len(filled)
    return call(
        functools.partial(later_body, half_heads, scale, extra),
        at,
        (rows // block,),
        [mine, mine, pl.BlockSpec((half_heads, DH, DH), lambda i, s: (0, 0, 0)), own, own]
        + [pl.BlockSpec(memory_space=pl.ANY)] * extra,
        [mine, mine],
        [sds((rows, width), F32)] * 2,
        4 * rows * DH * DH * half_heads,
        rows * DH * half_heads * 20,
        {6 + n: n for n in range(extra)},
        after=after,
        vmem=24,
    )(table, k, v, later, dk, dv, *filled)


def tie(array, *others):
    return lax.optimization_barrier((array,) + others)


def swap(array, axis, bit):
    size = lax.axis_size(axis)
    return lax.ppermute(array, axis, [(i, i ^ (1 << bit)) for i in range(size)])


def scan_states(theirs, mine, ctx_bits, flipped, fill):
    chunks = range(len(mine))
    pos = lax.axis_index("ctx")
    if flipped:
        pos = lax.axis_size("ctx") - 1 - pos
    held = []

    def beside(step, sent):
        got = [swap(array, "ctx", step) for array in sent]
        for n in chunks:
            done = fill[step, n]([sent[n], *held]) if (step, n) in fill else held
            got[n], *held[:] = tie(got[n], *done)
        return [array.astype(F32) for array in got]

    got = beside(0, theirs)
    own = [array.astype(F32) for array in mine]
    total = [own[n] + got[n] for n in chunks]
    prefix = [jnp.zeros_like(array) for array in total]
    for bit in range(1, ctx_bits):
        other = beside(bit, [array.astype(BF16) for array in total])
        before = (pos >> bit) & 1 == 1
        prefix = [prefix[n] + jnp.where(before, other[n], 0.0) for n in chunks]
        total = [total[n] + other[n] for n in chunks]
    upper = pos & 1 == 1
    mine_prefix = [(prefix[n] + jnp.where(upper, got[n], 0.0)).astype(BF16) for n in chunks]
    crossed = []
    for n in chunks:
        sent = (prefix[n] + jnp.where(upper, 0.0, own[n])).astype(BF16)
        if crossed:
            sent, crossed[-1], *held[:] = tie(sent, crossed[-1], *held)
        crossed.append(swap(sent, "ctx", 0))
        if (ctx_bits, n) in fill:
            held[:] = fill[ctx_bits, n]([sent, *held])
    return mine_prefix, crossed, held


def cuts_of(tiles, sizes):
    ends, at = [], 0
    for size in sizes:
        at = min(at + size, tiles)
        ends.append(at)
    ends[-1] = tiles
    starts = [0] + ends[:-1]
    return [(lo, hi) for lo, hi in zip(starts, ends) if lo < hi]


def on_device(queries, keys, values, teacher, out_weight, valid):
    rows, width = queries.shape
    heads = width // DH
    half_heads = heads // 2
    ctx_size = lax.axis_size("ctx")
    ctx_bits = ctx_size.bit_length() - 1
    chips = lax.axis_size("head") // 2
    ctx_id, head_id = lax.axis_index("ctx"), lax.axis_index("head")
    chip, core = head_id // 2, head_id % 2
    scale = 1.0 / math.sqrt(DH * rows * ctx_size)
    piece_width = teacher.shape[1]
    tile = 256 if piece_width % 256 == 0 else 128
    tiles = piece_width // tile
    sum_spans = [(lo * tile, hi * tile) for lo, hi in cuts_of(tiles, (2, 2, 1))]
    error_spans = [(lo * tile, hi * tile) for lo, hi in cuts_of(tiles, (3, 2))]

    my_half = ctx_id & 1
    entries = [my_half, 1 - my_half]
    for by in range(chips):
        for of_core in (core, 1 - core):
            device = lax.rem(chip + by, chips) * 2 + of_core
            entries.append(device * (piece_width // 128))
    table = [entry.astype(jnp.int32)[None] for entry in entries]
    mine_ix, theirs_ix = (0, 0), (1, 0)

    def column(by, crossed, lo):
        return 2 + 2 * (by % chips) + crossed, lo // 128


    chunks = 2 if half_heads % 2 == 0 else 1
    chunk_heads = half_heads // chunks
    last_step = ctx_bits - 1

    kv_theirs = kv_states(table, [theirs_ix], keys, values, chunk_heads, chunks)
    kv_mine = kv_states(table, [mine_ix], keys, values, chunk_heads, chunks, [kv_theirs[0]])
    parts, counts = {}, {}

    def intra_of(name, half):
        def run(after):
            parts[name] = intra(table, [half], queries, keys, values, half_heads, after)
            return [parts[name]]

        return run

    def first_fill(after):
        counts["own"], *after = tie(jnp.full((8, 128), jnp.sum(valid), jnp.int32), *after)
        got = swap(counts["own"], "ctx", 0)
        after = intra_of("mine", mine_ix)(after)
        got, *after = tie(got, *after)
        counts["pair"] = counts["own"] + got
        if last_step > 1:
            counts["got"] = swap(counts["pair"], "ctx", 1)
        return after

    def last_fill(after):
        if "own" not in counts:
            after = first_fill(after)
        after = intra_of("theirs", theirs_ix)(after)
        count = counts["pair"]
        for bit in range(1, last_step):
            got = counts["got"] if bit == 1 else swap(count, "ctx", bit)
            got, *after = tie(got, *after)
            count = count + got
        return [*after, count]

    if chunks > 1:
        fill = {(last_step, 0): first_fill, (ctx_bits, 0): last_fill}
    else:
        fill = {(last_step, 0): last_fill}
    before_mine, before_theirs, (*_, count) = scan_states(
        kv_theirs, kv_mine, ctx_bits, False, fill
    )
    count = count + swap(count, "ctx", last_step)
    before_theirs[-1], count = tie(before_theirs[-1], count)
    other_weight = swap(out_weight, "head", 0)

    def both_cores(array):
        return array, swap(array, "head", 0)

    attn_mine = both_cores(
        attend(table, [mine_ix], scale, queries, parts["mine"], before_mine)
    )
    attn_theirs = both_cores(
        attend(table, [theirs_ix], scale, queries, parts["theirs"], before_theirs)
    )

    def terms(by, lo, hi, after=()):
        at = [mine_ix, theirs_ix, column(by, 0, lo)]
        return project(
            table, at, attn_mine, attn_theirs, out_weight, other_weight, hi - lo, after
        )

    def shift(array, by):
        size = 2 * chips
        return lax.ppermute(array, "head", [(i, (i + 2 * by) % size) for i in range(size)])

    arrived, own, after = [], [], []
    first = sum_spans[0][1]
    for n, (lo, hi) in enumerate(sum_spans):
        got = []
        if n == 1:
            own.append(terms(0, 0, first, after))
            after = [own[0]]
        if n == 2:
            after = after + arrived[0]
        for by in range(1, chips):
            summed = terms(by, lo, hi, after)
            after = [summed]
            got.append(shift(summed, by))
        arrived.append(got)
    if first < piece_width:
        own.append(terms(0, first, piece_width, after))
    else:
        own.append(terms(0, 0, piece_width, after))
    own_spans = [(0, first), (first, piece_width)] if len(own) > 1 else [(0, piece_width)]

    factor = rows * ctx_size / count[0, 0].astype(F32)
    weigh = (valid.astype(F32) * factor)[:, None]

    def columns(pieces, spans, lo, hi):
        inside = [
            piece[:, max(lo - base, 0) : hi - base].astype(F32)
            for (base, end), piece in zip(spans, pieces)
            if base < hi and lo < end
        ]
        return jnp.concatenate(inside, 1)

    def error_of(lo, hi):
        predicted = columns(own, own_spans, lo, hi)
        for by in range(1, chips):
            predicted = predicted + columns([got[by - 1] for got in arrived], sum_spans, lo, hi)
        return (weigh * (predicted - teacher[:, lo:hi].astype(F32))).astype(BF16)

    errors = [error_of(lo, hi) for lo, hi in error_spans]
    near = [errors, [swap(error, "head", 0) for error in errors]]
    states = {
        "theirs": jnp.concatenate(before_theirs),
        "mine": jnp.concatenate(before_mine),
    }
    acc, summed_near = grad_accumulate(
        table, [column(0, 0, 0), column(0, 1, 0)], near, None, out_weight, list(states.values())
    )

    early = max(1, len(error_spans) - 1)
    gathered = [[shift(error, by) for by in range(1, chips)] for error in errors]

    def sources(select, token, lo):
        groups, at = [], []
        for by in range(1, chips):
            pieces = [got[by - 1] for got in gathered[select]]
            *late, token = tie(pieces[0], *pieces[1:], token)
            groups += [pieces, [swap(piece, "head", 0) for piece in late]]
            at += [column(chips - by, 0, lo), column(chips - by, 1, lo)]
        return groups, at, token

    last, last_at, token = [], [], summed_near
    if chips > 1:
        far, at, token = sources(slice(0, early), summed_near, 0)
        acc, summed_far = grad_accumulate(table, at, far, acc, out_weight, [token])
        last, last_at, token = sources(slice(early, None), summed_far, error_spans[early][0])

    def last_of(half, after=()):
        return grad_last(table, [half, *last_at], acc, queries, last, out_weight, half_heads, after)

    g_theirs, r_theirs = last_of(theirs_ix, [token])
    g_mine, r_mine = last_of(mine_ix, [r_theirs])
    done_q, done_kv = [], {"theirs": [], "mine": []}
    halves = {"theirs": (theirs_ix, g_theirs), "mine": (mine_ix, g_mine)}

    def back(name, lo, hi, after):
        half, g = halves[name]
        *got, token = back_local(
            table, [half], (lo, hi), scale, queries, keys, values, g, states[name],
            done_q + done_kv[name], half_heads, after,
        )
        done_q[:], done_kv[name] = got[:1], got[1:]
        return [token]

    groups = half_heads // math.gcd(half_heads, 2)
    split = max(1, groups * 3 // 4)
    order = [("mine", 0, split), ("theirs", 0, groups), ("mine", split, groups)]

    def beside_backward(step):
        def run(after):
            if step == 0:
                return [r_mine]
            todo = order[: step if step < 3 else 0]
            del order[: len(todo)]
            for name, lo, hi in todo:
                if lo < hi:
                    after = back(name, lo, hi, after)
            return after

        return run

    (later_mine,), (later_theirs,), token = scan_states(
        [r_theirs], [r_mine], ctx_bits, True,
        {(n, 0): beside_backward(n) for n in range(ctx_bits)},
    )
    token = [*token, later_mine]
    for name, lo, hi in order:
        if lo < hi:
            token = back(name, lo, hi, token)
    (q_grad,) = done_q
    grads = add_later(
        table, [mine_ix], scale, keys, values, later_mine, *done_kv["mine"], [], half_heads, token
    )
    k_grad, v_grad = add_later(
        table, [theirs_ix], scale, keys, values, later_theirs, *done_kv["theirs"], list(grads),
        half_heads, [],
    )
    return q_grad, k_grad, v_grad


def solution(mesh):
    in_specs = (
        P("ctx", "head"),
        P("ctx", "head"),
        P("ctx", "head"),
        P("ctx", "head"),
        P("head", None),
        P("ctx"),
    )
    out_specs = (P("ctx", "head"), P("ctx", "head"), P("ctx", "head"))
    return jax.shard_map(
        on_device, mesh=mesh, in_specs=in_specs, out_specs=out_specs, check_vma=False
    )
```

```python
import functools
import math

import jax
import jax.numpy as jnp
from jax import lax
from jax.experimental import pallas as pl
from jax.experimental.pallas import tpu as pltpu
from jax.sharding import PartitionSpec as P

DH = 128
GROUP = 4
HINT = 1000000000000
NT = (((1,), (1,)), ((), ()))
TN = (((0,), (0,)), ((), ()))
F32 = jnp.float32
BF16 = jnp.bfloat16


def dot(a, b, dims=(((1,), (0,)), ((), ()))):
    return lax.dot_general(a, b, dims, preferred_element_type=F32)


class Entries:
    def __init__(self, refs, at):
        self.refs, self.at = refs, at

    def __getitem__(self, n):
        if not isinstance(n, int):
            return jnp.where(n == 0, self[0], self[1])
        more = self.at[n][1]
        return self.refs[n][0] + more if more else self.refs[n][0]


def call(body, at, grid, in_specs, out_specs, out_shape, flops, moved, aliases=None, after=(), vmem=40, scratch=(), token=False):
    count = len(in_specs)
    many = isinstance(out_specs, (list, tuple))
    if token:
        out_specs = [*out_specs, pl.BlockSpec((8, 128), lambda i, s: (0, 0))]
        out_shape = [*out_shape, sds((8, 128), F32)]

    def seen(spec):
        if spec.index_map is None:
            return spec
        index_map = spec.index_map
        return pl.BlockSpec(spec.block_shape, lambda i, *s: index_map(i, Entries(s, at)))

    in_specs = [seen(spec) for spec in in_specs]
    out_specs = [seen(spec) for spec in out_specs] if many else seen(out_specs)

    def ordered(*refs):
        scalars, refs = refs[: len(at)], list(refs[len(at) :])
        if token:
            refs.pop(count + len(after) + len(out_shape) - 1)[...] = jnp.zeros((8, 128), F32)
        body(Entries(scalars, at), *refs[:count], *refs[count + len(after) :])

    kernel = pl.pallas_call(
        ordered,
        grid_spec=pltpu.PrefetchScalarGridSpec(
            num_scalar_prefetch=len(at),
            grid=grid,
            in_specs=list(in_specs) + [pl.BlockSpec(memory_space=pl.ANY)] * len(after),
            out_specs=out_specs,
            scratch_shapes=list(scratch),
        ),
        out_shape=out_shape,
        input_output_aliases={n + len(at) - 1: m for n, m in (aliases or {}).items()},
        compiler_params=pltpu.CompilerParams(vmem_limit_bytes=vmem * 1024 * 1024),
        cost_estimate=pl.CostEstimate(
            flops=max(1, flops // HINT), bytes_accessed=max(1, moved // HINT), transcendentals=0
        ),
    )
    return lambda table, *args: kernel(*(table[n] for n, _ in at), *args, *after)


def in_hbm(array):
    return pltpu.with_memory_space_constraint(array, pltpu.HBM)


def sds(shape, dtype):
    return jax.ShapeDtypeStruct(shape, dtype)


def lower_mask(n):
    rows = lax.broadcasted_iota(jnp.int32, (n, n), 0)
    cols = lax.broadcasted_iota(jnp.int32, (n, n), 1)
    return rows >= cols


def cut(i):
    return slice(i * DH, (i + 1) * DH)


def group_of(half_heads):
    return math.gcd(half_heads, GROUP)


def kv_body(group, chunks, idx, k, v, *outs):
    for n, out in enumerate(outs):

        @pl.when(pl.program_id(0) == n)
        def _(out=out):
            for i in range(group):
                out[i] = dot(k[:, cut(i)], v[:, cut(i)], TN).astype(BF16)


def kv_states(table, at, k, v, heads, chunks, after=()):
    rows = k.shape[0]
    blk = pl.BlockSpec((rows, heads * DH), lambda i, s: (0, s[0] * chunks + i))
    return call(
        functools.partial(kv_body, heads, chunks),
        at,
        (chunks,),
        [blk, blk],
        [pl.BlockSpec((heads, DH, DH), lambda i, s: (0, 0, 0))] * chunks,
        [sds((heads, DH, DH), BF16)] * chunks,
        2 * rows * DH * DH * heads * chunks,
        rows * DH * heads * chunks * 4,
        after=after,
        vmem=30,
    )(table, in_hbm(k), in_hbm(v))


def intra_body(group, block, idx, q, k, v, out):
    mask = lower_mask(block)
    n = q.shape[0] // block
    for i in range(group):
        c = cut(i)
        state = None
        for b in range(n):
            r = slice(b * block, (b + 1) * block)
            qb, kb, vb = q[r, c], k[r, c], v[r, c]
            s = jnp.where(mask, dot(qb, kb, NT), 0.0).astype(BF16)
            o = dot(s, vb)
            if state is not None:
                o = o + dot(qb, state.astype(BF16))
            if b < n - 1:
                kv = dot(kb, vb, TN)
                state = kv if state is None else state + kv
            out[r, c] = o


def intra(table, at, q, k, v, half_heads, after):
    rows = k.shape[0]
    block = math.gcd(rows, 256)
    group = group_of(half_heads)
    steps = half_heads // group
    blk = pl.BlockSpec((rows, group * DH), lambda i, s: (0, s[0] * steps + i))
    return call(
        functools.partial(intra_body, group, block),
        at,
        (steps,),
        [blk, blk, blk],
        [pl.BlockSpec((rows, group * DH), lambda i, s: (0, i))],
        [pltpu.HBM((rows, half_heads * DH), F32)],
        4 * rows * (block + DH) * DH * half_heads,
        rows * DH * half_heads * 10,
        after=after,
        vmem=30,
        token=True,
    )(table, in_hbm(q), in_hbm(k), in_hbm(v))


def attn_body(heads, scale, idx, q, part, *refs):
    *states, out = refs
    for n, state in enumerate(states):

        @pl.when(pl.program_id(0) == n)
        def _(state=state):
            for i in range(heads):
                c = cut(i)
                out[:, c] = (scale * (part[:, c] + dot(q[:, c], state[i]))).astype(BF16)


def attend(table, at, scale, q, part, states, after=()):
    rows = q.shape[0]
    chunks, heads = len(states), states[0].shape[0]
    blk = pl.BlockSpec((rows, heads * DH), lambda i, s: (0, i))
    return call(
        functools.partial(attn_body, heads, scale),
        at,
        (chunks,),
        [
            pl.BlockSpec((rows, heads * DH), lambda i, s: (0, s[0] * chunks + i)),
            blk,
        ]
        + [pl.BlockSpec((heads, DH, DH), lambda i, s: (0, 0, 0))] * chunks,
        blk,
        sds((rows, chunks * heads * DH), BF16),
        2 * rows * DH * DH * heads * chunks,
        rows * DH * heads * chunks * 8,
        after=after,
    )(table, q, part, *states)


def project_body(idx, a0, b0, a1, b1, w, wo, out, acc):
    i = pl.program_id(0)

    @pl.when(i == 0)
    def _():
        acc[...] = dot(a0[...], w[...]) + dot(b0[...], wo[...])

    @pl.when(i == 1)
    def _():
        out[...] = (acc[...] + dot(a1[...], w[...]) + dot(b1[...], wo[...])).astype(BF16)


def project(table, at, mine, theirs, weight, other_weight, span, after=()):
    rows, depth = mine[0].shape
    whole = pl.BlockSpec((rows, depth), lambda i, s: (0, 0))
    return call(
        project_body,
        at,
        (2,),
        [
            whole,
            whole,
            whole,
            whole,
            pl.BlockSpec(
                (pl.Element(depth), pl.Element(span)), lambda i, s: (s[i] * depth, s[2] * 128)
            ),
            pl.BlockSpec(
                (pl.Element(depth), pl.Element(span)), lambda i, s: (s[i] * depth, s[2] * 128)
            ),
        ],
        pl.BlockSpec((rows, span), lambda i, s: (0, 0)),
        sds((rows, span), BF16),
        8 * rows * depth * span,
        8 * depth * span + 8 * rows * depth + 2 * rows * span,
        after=after,
        vmem=44,
        scratch=[pltpu.VMEM((rows, span), F32)],
    )(table, *mine, *theirs, weight, other_weight)


def grad_body(counts, with_acc, idx, *refs):
    refs = list(refs)
    acc = refs.pop(0)[...] if with_acc else None
    out = refs.pop()
    for count in counts:
        w, lo = refs[count], 0
        for piece in refs[:count]:
            hi = lo + piece.shape[1]
            t = dot(piece[...], w[:, lo:hi], NT)
            acc = t if acc is None else acc + t
            lo = hi
        refs = refs[count + 1 :]
    out[...] = acc


def grad_accumulate(table, at, groups, acc, weight, after=()):
    depth = weight.shape[0]
    rows = groups[0][0].shape[0]
    row_tile = math.gcd(depth, 512)
    in_specs, args = [], []
    if acc is not None:
        in_specs.append(pl.BlockSpec((rows, row_tile), lambda i, s: (0, i)))
        args.append(in_hbm(acc))
    total = 0
    for g, pieces in enumerate(groups):
        span = sum(piece.shape[1] for piece in pieces)
        total += span
        in_specs += [pl.BlockSpec(piece.shape, lambda i, s: (0, 0)) for piece in pieces]
        in_specs.append(
            pl.BlockSpec(
                (pl.Element(row_tile), pl.Element(span)),
                lambda i, s, g=g: (i * row_tile, s[g] * 128),
            )
        )
        args += [*pieces, weight]
    return call(
        functools.partial(grad_body, [len(pieces) for pieces in groups], acc is not None),
        at,
        (depth // row_tile,),
        in_specs,
        [pl.BlockSpec((rows, row_tile), lambda i, s: (0, i))],
        [pltpu.HBM((rows, depth), F32)],
        2 * rows * depth * total,
        2 * depth * total + 8 * rows * depth,
        None,
        after=after,
        vmem=44,
        token=True,
    )(table, *args)


def last_body(group, counts, idx, acc, q, *refs):
    *refs, g_out, r_out, held, sems = refs
    i = pl.program_id(0)
    wide = held.shape[2]
    steps = held.shape[0]

    def fetch(n):
        start = pl.multiple_of((idx[0] * steps + n) * wide, wide)
        return pltpu.make_async_copy(acc.at[:, pl.ds(start, wide)], held.at[n], sems.at[n])

    @pl.when(i == 0)
    def _():
        for n in range(steps):
            fetch(n).start()

    t = None
    for count in counts:
        w, lo = refs[count], 0
        for piece in refs[:count]:
            hi = lo + piece.shape[1]
            u = dot(piece[...], w[:, lo:hi], NT)
            t = u if t is None else t + u
            lo = hi
        refs = refs[count + 1 :]
    fetch(i).wait()
    t = held[i] if t is None else t + held[i]
    g = t.astype(BF16)
    g_out[...] = g
    for i in range(group):
        r_out[i] = dot(q[:, cut(i)], g[:, cut(i)], TN).astype(BF16)


def grad_last(table, at, acc, q, groups, weight, half_heads, after=()):
    rows = acc.shape[0]
    group = group_of(half_heads)
    steps = half_heads // group
    wide = group * DH
    mine = pl.BlockSpec((rows, wide), lambda i, s: (0, s[0] * steps + i))
    in_specs, total = [pl.BlockSpec(memory_space=pltpu.HBM), mine], 0
    args = [in_hbm(acc), q]
    for n, pieces in enumerate(groups):
        span = sum(piece.shape[1] for piece in pieces)
        total += span
        in_specs += [pl.BlockSpec(piece.shape, lambda i, s: (0, 0)) for piece in pieces]
        in_specs.append(
            pl.BlockSpec(
                (pl.Element(wide), pl.Element(span)),
                lambda i, s, n=n: ((s[0] * steps + i) * wide, s[1 + n] * 128),
            )
        )
        args += [*pieces, weight]
    return call(
        functools.partial(last_body, group, [len(pieces) for pieces in groups]),
        at,
        (steps,),
        in_specs,
        [
            pl.BlockSpec((rows, wide), lambda i, s: (0, i)),
            pl.BlockSpec((group, DH, DH), lambda i, s: (i, 0, 0)),
        ],
        [pltpu.HBM((rows, half_heads * DH), BF16), sds((half_heads, DH, DH), BF16)],
        2 * rows * half_heads * DH * (total + DH),
        half_heads * DH * (rows * 8 + 2 * total),
        after=after,
        vmem=44,
        scratch=[
            pltpu.VMEM((steps, rows, wide), F32),
            pltpu.SemaphoreType.DMA((steps,)),
        ],
    )(table, *args)


def back_body(group, block, scale, extra, idx, q, k, v, g, state, *refs):
    dq, dk, dv = refs[extra:]
    mask = lower_mask(block)
    n = q.shape[0] // block
    for i in range(group):
        c = cut(i)
        before = state[i].astype(F32)
        later = None
        dks, dvs = [], []
        for b in range(n):
            r = slice(b * block, (b + 1) * block)
            qb, kb, vb, gb = q[r, c], k[r, c], v[r, c], g[r, c]
            gs = jnp.where(mask, dot(gb, vb, NT), 0.0).astype(BF16)
            s = jnp.where(mask, dot(qb, kb, NT), 0.0).astype(BF16)
            dq[r, c] = scale * (dot(gs, kb) + dot(gb, before.astype(BF16), NT))
            dks.append(dot(gs, qb, TN))
            dvs.append(dot(s, gb, TN))
            if b < n - 1:
                before = before + dot(kb, vb, TN)
        for b in reversed(range(n)):
            r = slice(b * block, (b + 1) * block)
            qb, kb, vb, gb = q[r, c], k[r, c], v[r, c], g[r, c]
            dkb, dvb = dks[b], dvs[b]
            if later is not None:
                lb = later.astype(BF16)
                dkb = dkb + dot(vb, lb, NT)
                dvb = dvb + dot(kb, lb)
            dk[r, c] = dkb.astype(dk.dtype)
            dv[r, c] = dvb.astype(dv.dtype)
            if b > 0:
                qg = dot(qb, gb, TN)
                later = qg if later is None else later + qg


def back_local(table, at, pairs, scale, q, k, v, g, state, filled, half_heads, after):
    rows, width = q.shape
    block = math.gcd(rows, 256)
    group = math.gcd(half_heads, 2)
    first, steps = pairs[0], pairs[1] - pairs[0]
    heads = group * steps
    wide = group * DH
    mine = pl.BlockSpec((rows, wide), lambda i, s: (0, s[0] * (half_heads // group) + first + i))
    own = pl.BlockSpec((rows, wide), lambda i, s: (0, first + i))
    extra = len(filled)
    half = pltpu.HBM((rows, half_heads * DH), BF16)
    return call(
        functools.partial(back_body, group, block, scale, extra),
        at,
        (steps,),
        [
            mine,
            mine,
            mine,
            own,
            pl.BlockSpec((group, DH, DH), lambda i, s: (first + i, 0, 0)),
        ]
        + [pl.BlockSpec(memory_space=pl.ANY)] * extra,
        [mine, own, own],
        [pltpu.HBM((rows, width), F32), half, half],
        2 * rows * DH * (5 * block + 4 * DH) * heads,
        rows * DH * heads * 20,
        {6 + n: n for n in range(extra)},
        after=after,
        vmem=30,
        token=True,
    )(table, in_hbm(q), in_hbm(k), in_hbm(v), in_hbm(g), state, *filled)


def later_body(heads, scale, extra, idx, k, v, later, dk_in, dv_in, *refs):
    dk, dv = refs[extra:]
    for i in range(heads):
        c = cut(i)
        dk[:, c] = scale * (dk_in[:, c] + dot(v[:, c], later[i], NT))
        dv[:, c] = scale * (dv_in[:, c] + dot(k[:, c], later[i]))


def add_later(table, at, scale, k, v, later, dk, dv, filled, half_heads, after):
    rows, width = k.shape
    block = math.gcd(rows, 256)
    wide = half_heads * DH
    mine = pl.BlockSpec((block, wide), lambda i, s: (i, s[0]))
    own = pl.BlockSpec((block, wide), lambda i, s: (i, 0))
    extra = len(filled)
    return call(
        functools.partial(later_body, half_heads, scale, extra),
        at,
        (rows // block,),
        [mine, mine, pl.BlockSpec((half_heads, DH, DH), lambda i, s: (0, 0, 0)), own, own]
        + [pl.BlockSpec(memory_space=pl.ANY)] * extra,
        [mine, mine],
        [sds((rows, width), F32)] * 2,
        4 * rows * DH * DH * half_heads,
        rows * DH * half_heads * 20,
        {6 + n: n for n in range(extra)},
        after=after,
        vmem=24,
    )(table, k, v, later, dk, dv, *filled)


def tie(array, *others):
    return lax.optimization_barrier((array,) + others)


def swap(array, axis, bit):
    size = lax.axis_size(axis)
    return lax.ppermute(array, axis, [(i, i ^ (1 << bit)) for i in range(size)])


def scan_states(theirs, mine, ctx_bits, flipped, fill):
    chunks = range(len(mine))
    pos = lax.axis_index("ctx")
    if flipped:
        pos = lax.axis_size("ctx") - 1 - pos
    held = []

    def beside(step, sent):
        got = [swap(array, "ctx", step) for array in sent]
        for n in chunks:
            done = fill[step, n]([sent[n], *held]) if (step, n) in fill else held
            got[n], *held[:] = tie(got[n], *done)
        return [array.astype(F32) for array in got]

    got = beside(0, theirs)
    own = [array.astype(F32) for array in mine]
    total = [own[n] + got[n] for n in chunks]
    prefix = [jnp.zeros_like(array) for array in total]
    for bit in range(1, ctx_bits):
        other = beside(bit, [array.astype(BF16) for array in total])
        before = (pos >> bit) & 1 == 1
        prefix = [prefix[n] + jnp.where(before, other[n], 0.0) for n in chunks]
        total = [total[n] + other[n] for n in chunks]
    upper = pos & 1 == 1
    mine_prefix = [(prefix[n] + jnp.where(upper, got[n], 0.0)).astype(BF16) for n in chunks]
    crossed = []
    for n in chunks:
        sent = (prefix[n] + jnp.where(upper, 0.0, own[n])).astype(BF16)
        if crossed:
            sent, crossed[-1], *held[:] = tie(sent, crossed[-1], *held)
        crossed.append(swap(sent, "ctx", 0))
        if (ctx_bits, n) in fill:
            held[:] = fill[ctx_bits, n]([sent, *held])
    return mine_prefix, crossed, held


def cuts_of(tiles, sizes):
    ends, at = [], 0
    for size in sizes:
        at = min(at + size, tiles)
        ends.append(at)
    ends[-1] = tiles
    starts = [0] + ends[:-1]
    return [(lo, hi) for lo, hi in zip(starts, ends) if lo < hi]


def on_device(queries, keys, values, teacher, out_weight, valid):
    rows, width = queries.shape
    heads = width // DH
    half_heads = heads // 2
    ctx_size = lax.axis_size("ctx")
    ctx_bits = ctx_size.bit_length() - 1
    chips = lax.axis_size("head") // 2
    ctx_id, head_id = lax.axis_index("ctx"), lax.axis_index("head")
    chip, core = head_id // 2, head_id % 2
    scale = 1.0 / math.sqrt(DH * rows * ctx_size)
    piece_width = teacher.shape[1]
    tile = 256 if piece_width % 256 == 0 else 128
    tiles = piece_width // tile
    sum_spans = [(lo * tile, hi * tile) for lo, hi in cuts_of(tiles, (2, 2, 1))]
    error_spans = [(lo * tile, hi * tile) for lo, hi in cuts_of(tiles, (3, 2))]

    my_half = ctx_id & 1
    entries = [my_half, 1 - my_half]
    for by in range(chips):
        for of_core in (core, 1 - core):
            device = lax.rem(chip + by, chips) * 2 + of_core
            entries.append(device * (piece_width // 128))
    table = [entry.astype(jnp.int32)[None] for entry in entries]
    mine_ix, theirs_ix = (0, 0), (1, 0)

    def column(by, crossed, lo):
        return 2 + 2 * (by % chips) + crossed, lo // 128


    chunks = 2 if half_heads % 2 == 0 else 1
    chunk_heads = half_heads // chunks
    last_step = ctx_bits - 1

    kv_theirs = kv_states(table, [theirs_ix], keys, values, chunk_heads, chunks)
    kv_mine = kv_states(table, [mine_ix], keys, values, chunk_heads, chunks, [kv_theirs[0]])
    parts, counts = {}, {}

    def intra_of(name, half):
        def run(after):
            parts[name], token = intra(
                table, [half], queries, keys, values, half_heads, after
            )
            return [token]

        return run

    def first_fill(after):
        counts["own"], *after = tie(jnp.full((8, 128), jnp.sum(valid), jnp.int32), *after)
        got = swap(counts["own"], "ctx", 0)
        after = intra_of("mine", mine_ix)(after)
        got, *after = tie(got, *after)
        counts["pair"] = counts["own"] + got
        if last_step > 1:
            counts["got"] = swap(counts["pair"], "ctx", 1)
        return after

    def last_fill(after):
        if "own" not in counts:
            after = first_fill(after)
        after = intra_of("theirs", theirs_ix)(after)
        count = counts["pair"]
        for bit in range(1, last_step):
            got = counts["got"] if bit == 1 else swap(count, "ctx", bit)
            got, *after = tie(got, *after)
            count = count + got
        return [*after, count]

    if chunks > 1:
        fill = {(last_step, 0): first_fill, (ctx_bits, 0): last_fill}
    else:
        fill = {(last_step, 0): last_fill}
    before_mine, before_theirs, (*held, count) = scan_states(
        kv_theirs, kv_mine, ctx_bits, False, fill
    )
    count = count + swap(count, "ctx", last_step)
    before_theirs[-1], count = tie(before_theirs[-1], count)
    other_weight = swap(out_weight, "head", 0)

    def both_cores(array):
        return array, swap(array, "head", 0)

    attn_mine = both_cores(
        attend(table, [mine_ix], scale, queries, parts["mine"], before_mine)
    )
    attn_theirs = both_cores(
        attend(table, [theirs_ix], scale, queries, parts["theirs"], before_theirs, held)
    )

    def terms(by, lo, hi, after=()):
        at = [mine_ix, theirs_ix, column(by, 0, lo)]
        return project(
            table, at, attn_mine, attn_theirs, out_weight, other_weight, hi - lo, after
        )

    def shift(array, by):
        size = 2 * chips
        return lax.ppermute(array, "head", [(i, (i + 2 * by) % size) for i in range(size)])

    arrived, own, after = [], [], []
    first = sum_spans[0][1]
    for n, (lo, hi) in enumerate(sum_spans):
        got = []
        if n == 1:
            own.append(terms(0, 0, first, after))
            after = [own[0]]
        if n == 2:
            after = after + arrived[0]
        for by in range(1, chips):
            summed = terms(by, lo, hi, after)
            after = [summed]
            got.append(shift(summed, by))
        arrived.append(got)
    if first < piece_width:
        own.append(terms(0, first, piece_width, after))
    else:
        own.append(terms(0, 0, piece_width, after))
    own_spans = [(0, first), (first, piece_width)] if len(own) > 1 else [(0, piece_width)]

    factor = rows * ctx_size / count[0, 0].astype(F32)
    weigh = (valid.astype(F32) * factor)[:, None]

    def columns(pieces, spans, lo, hi):
        inside = [
            piece[:, max(lo - base, 0) : hi - base].astype(F32)
            for (base, end), piece in zip(spans, pieces)
            if base < hi and lo < end
        ]
        return jnp.concatenate(inside, 1)

    def error_of(lo, hi):
        predicted = columns(own, own_spans, lo, hi)
        for by in range(1, chips):
            predicted = predicted + columns([got[by - 1] for got in arrived], sum_spans, lo, hi)
        return (weigh * (predicted - teacher[:, lo:hi].astype(F32))).astype(BF16)

    errors = [error_of(lo, hi) for lo, hi in error_spans]
    near = [errors, [swap(error, "head", 0) for error in errors]]
    states = {
        "theirs": jnp.concatenate(before_theirs),
        "mine": jnp.concatenate(before_mine),
    }
    acc, summed_near = grad_accumulate(
        table, [column(0, 0, 0), column(0, 1, 0)], near, None, out_weight, list(states.values())
    )

    early = max(1, len(error_spans) - 1)
    gathered = [[shift(error, by) for by in range(1, chips)] for error in errors]

    def sources(select, token, lo):
        groups, at = [], []
        for by in range(1, chips):
            pieces = [got[by - 1] for got in gathered[select]]
            *late, token = tie(pieces[0], *pieces[1:], token)
            groups += [pieces, [swap(piece, "head", 0) for piece in late]]
            at += [column(chips - by, 0, lo), column(chips - by, 1, lo)]
        return groups, at, token

    last, last_at, token = [], [], summed_near
    if chips > 1:
        far, at, token = sources(slice(0, early), summed_near, 0)
        acc, summed_far = grad_accumulate(table, at, far, acc, out_weight, [token])
        last, last_at, token = sources(slice(early, None), summed_far, error_spans[early][0])

    def last_of(half, after=()):
        return grad_last(table, [half, *last_at], acc, queries, last, out_weight, half_heads, after)

    g_theirs, r_theirs = last_of(theirs_ix, [token])
    g_mine, r_mine = last_of(mine_ix, [r_theirs])
    done_q, done_kv = [], {"theirs": [], "mine": []}
    halves = {"theirs": (theirs_ix, g_theirs), "mine": (mine_ix, g_mine)}

    def back(name, lo, hi, after):
        half, g = halves[name]
        *got, token = back_local(
            table, [half], (lo, hi), scale, queries, keys, values, g, states[name],
            done_q + done_kv[name], half_heads, after,
        )
        done_q[:], done_kv[name] = got[:1], got[1:]
        return [token]

    groups = half_heads // math.gcd(half_heads, 2)
    split = max(1, groups * 3 // 4)
    order = [("mine", 0, split), ("theirs", 0, groups), ("mine", split, groups)]

    def beside_backward(step):
        def run(after):
            if step == 0:
                return [r_mine]
            todo = order[: step if step < 3 else 0]
            del order[: len(todo)]
            for name, lo, hi in todo:
                if lo < hi:
                    after = back(name, lo, hi, after)
            return after

        return run

    (later_mine,), (later_theirs,), token = scan_states(
        [r_theirs], [r_mine], ctx_bits, True,
        {(n, 0): beside_backward(n) for n in range(ctx_bits)},
    )
    token = [*token, later_mine]
    for name, lo, hi in order:
        if lo < hi:
            token = back(name, lo, hi, token)
    (q_grad,) = done_q
    grads = add_later(
        table, [mine_ix], scale, keys, values, later_mine, *done_kv["mine"], [], half_heads, token
    )
    k_grad, v_grad = add_later(
        table, [theirs_ix], scale, keys, values, later_theirs, *done_kv["theirs"], list(grads),
        half_heads, [],
    )
    return q_grad, k_grad, v_grad


def solution(mesh):
    in_specs = (
        P("ctx", "head"),
        P("ctx", "head"),
        P("ctx", "head"),
        P("ctx", "head"),
        P("head", None),
        P("ctx"),
    )
    out_specs = (P("ctx", "head"), P("ctx", "head"), P("ctx", "head"))
    return jax.shard_map(
        on_device, mesh=mesh, in_specs=in_specs, out_specs=out_specs, check_vma=False
    )
```

```python
import functools
import math

import jax
import jax.numpy as jnp
from jax import lax
from jax.experimental import pallas as pl
from jax.experimental.pallas import tpu as pltpu
from jax.sharding import PartitionSpec as P

DH = 128
GROUP = 4
HINT = 1000000000000
NT = (((1,), (1,)), ((), ()))
TN = (((0,), (0,)), ((), ()))
F32 = jnp.float32
BF16 = jnp.bfloat16


def dot(a, b, dims=(((1,), (0,)), ((), ()))):
    return lax.dot_general(a, b, dims, preferred_element_type=F32)


class Entries:
    def __init__(self, refs, at):
        self.refs, self.at = refs, at

    def __getitem__(self, n):
        if not isinstance(n, int):
            return jnp.where(n == 0, self[0], self[1])
        more = self.at[n][1]
        return self.refs[n][0] + more if more else self.refs[n][0]


def call(body, at, grid, in_specs, out_specs, out_shape, flops, moved, aliases=None, after=(), vmem=40, scratch=(), token=False):
    count = len(in_specs)
    many = isinstance(out_specs, (list, tuple))
    if token:
        out_specs = [*out_specs, pl.BlockSpec((8, 128), lambda i, s: (0, 0))]
        out_shape = [*out_shape, sds((8, 128), F32)]

    def seen(spec):
        if spec.index_map is None:
            return spec
        index_map = spec.index_map
        return pl.BlockSpec(spec.block_shape, lambda i, *s: index_map(i, Entries(s, at)))

    in_specs = [seen(spec) for spec in in_specs]
    out_specs = [seen(spec) for spec in out_specs] if many else seen(out_specs)

    def ordered(*refs):
        scalars, refs = refs[: len(at)], list(refs[len(at) :])
        if token:
            refs.pop(count + len(after) + len(out_shape) - 1)[...] = jnp.zeros((8, 128), F32)
        body(Entries(scalars, at), *refs[:count], *refs[count + len(after) :])

    kernel = pl.pallas_call(
        ordered,
        grid_spec=pltpu.PrefetchScalarGridSpec(
            num_scalar_prefetch=len(at),
            grid=grid,
            in_specs=list(in_specs) + [pl.BlockSpec(memory_space=pl.ANY)] * len(after),
            out_specs=out_specs,
            scratch_shapes=list(scratch),
        ),
        out_shape=out_shape,
        input_output_aliases={n + len(at) - 1: m for n, m in (aliases or {}).items()},
        compiler_params=pltpu.CompilerParams(vmem_limit_bytes=vmem * 1024 * 1024),
        cost_estimate=pl.CostEstimate(
            flops=max(1, flops // HINT), bytes_accessed=max(1, moved // HINT), transcendentals=0
        ),
    )
    return lambda table, *args: kernel(*(table[n] for n, _ in at), *args, *after)


def in_hbm(array):
    return pltpu.with_memory_space_constraint(array, pltpu.HBM)


def sds(shape, dtype):
    return jax.ShapeDtypeStruct(shape, dtype)


def lower_mask(n):
    rows = lax.broadcasted_iota(jnp.int32, (n, n), 0)
    cols = lax.broadcasted_iota(jnp.int32, (n, n), 1)
    return rows >= cols


def cut(i):
    return slice(i * DH, (i + 1) * DH)


def group_of(half_heads):
    return math.gcd(half_heads, GROUP)


def kv_body(group, chunks, idx, k, v, *outs):
    for n, out in enumerate(outs):

        @pl.when(pl.program_id(0) == n)
        def _(out=out):
            for i in range(group):
                out[i] = dot(k[:, cut(i)], v[:, cut(i)], TN).astype(BF16)


def kv_states(table, at, k, v, heads, chunks, after=()):
    rows = k.shape[0]
    blk = pl.BlockSpec((rows, heads * DH), lambda i, s: (0, s[0] * chunks + i))
    return call(
        functools.partial(kv_body, heads, chunks),
        at,
        (chunks,),
        [blk, blk],
        [pl.BlockSpec((heads, DH, DH), lambda i, s: (0, 0, 0))] * chunks,
        [sds((heads, DH, DH), BF16)] * chunks,
        2 * rows * DH * DH * heads * chunks,
        rows * DH * heads * chunks * 4,
        after=after,
        vmem=30,
    )(table, in_hbm(k), in_hbm(v))


def intra_body(group, block, idx, q, k, v, out):
    mask = lower_mask(block)
    n = q.shape[0] // block
    for i in range(group):
        c = cut(i)
        state = None
        for b in range(n):
            r = slice(b * block, (b + 1) * block)
            qb, kb, vb = q[r, c], k[r, c], v[r, c]
            s = jnp.where(mask, dot(qb, kb, NT), 0.0).astype(BF16)
            o = dot(s, vb)
            if state is not None:
                o = o + dot(qb, state.astype(BF16))
            if b < n - 1:
                kv = dot(kb, vb, TN)
                state = kv if state is None else state + kv
            out[r, c] = o


def intra(table, at, q, k, v, half_heads, after):
    rows = k.shape[0]
    block = math.gcd(rows, 256)
    group = group_of(half_heads)
    steps = half_heads // group
    blk = pl.BlockSpec((rows, group * DH), lambda i, s: (0, s[0] * steps + i))
    return call(
        functools.partial(intra_body, group, block),
        at,
        (steps,),
        [blk, blk, blk],
        [pl.BlockSpec((rows, group * DH), lambda i, s: (0, i))],
        [pltpu.HBM((rows, half_heads * DH), F32)],
        4 * rows * (block + DH) * DH * half_heads,
        rows * DH * half_heads * 10,
        after=after,
        vmem=30,
        token=True,
    )(table, in_hbm(q), in_hbm(k), in_hbm(v))


def attn_body(heads, scale, idx, q, part, *refs):
    *states, out = refs
    for n, state in enumerate(states):

        @pl.when(pl.program_id(0) == n)
        def _(state=state):
            for i in range(heads):
                c = cut(i)
                out[:, c] = (scale * (part[:, c] + dot(q[:, c], state[i]))).astype(BF16)


def attend(table, at, scale, q, part, states, after=()):
    rows = q.shape[0]
    chunks, heads = len(states), states[0].shape[0]
    blk = pl.BlockSpec((rows, heads * DH), lambda i, s: (0, i))
    return call(
        functools.partial(attn_body, heads, scale),
        at,
        (chunks,),
        [
            pl.BlockSpec((rows, heads * DH), lambda i, s: (0, s[0] * chunks + i)),
            blk,
        ]
        + [pl.BlockSpec((heads, DH, DH), lambda i, s: (0, 0, 0))] * chunks,
        blk,
        sds((rows, chunks * heads * DH), BF16),
        2 * rows * DH * DH * heads * chunks,
        rows * DH * heads * chunks * 8,
        after=after,
    )(table, q, part, *states)


def project_body(idx, a0, b0, a1, b1, w, wo, out, acc):
    i = pl.program_id(0)

    @pl.when(i == 0)
    def _():
        acc[...] = dot(a0[...], w[...]) + dot(b0[...], wo[...])

    @pl.when(i == 1)
    def _():
        out[...] = (acc[...] + dot(a1[...], w[...]) + dot(b1[...], wo[...])).astype(BF16)


def project(table, at, mine, theirs, weight, other_weight, span, after=()):
    rows, depth = mine[0].shape
    whole = pl.BlockSpec((rows, depth), lambda i, s: (0, 0))
    return call(
        project_body,
        at,
        (2,),
        [
            whole,
            whole,
            whole,
            whole,
            pl.BlockSpec(
                (pl.Element(depth), pl.Element(span)), lambda i, s: (s[i] * depth, s[2] * 128)
            ),
            pl.BlockSpec(
                (pl.Element(depth), pl.Element(span)), lambda i, s: (s[i] * depth, s[2] * 128)
            ),
        ],
        pl.BlockSpec((rows, span), lambda i, s: (0, 0)),
        sds((rows, span), BF16),
        8 * rows * depth * span,
        8 * depth * span + 8 * rows * depth + 2 * rows * span,
        after=after,
        vmem=44,
        scratch=[pltpu.VMEM((rows, span), F32)],
    )(table, *mine, *theirs, weight, other_weight)


def grad_body(counts, with_acc, idx, *refs):
    refs = list(refs)
    acc = refs.pop(0)[...] if with_acc else None
    out = refs.pop()
    for count in counts:
        w, lo = refs[count], 0
        for piece in refs[:count]:
            hi = lo + piece.shape[1]
            t = dot(piece[...], w[:, lo:hi], NT)
            acc = t if acc is None else acc + t
            lo = hi
        refs = refs[count + 1 :]
    out[...] = acc


def grad_accumulate(table, at, groups, acc, weight, after=()):
    depth = weight.shape[0]
    rows = groups[0][0].shape[0]
    row_tile = math.gcd(depth, 512)
    in_specs, args = [], []
    if acc is not None:
        in_specs.append(pl.BlockSpec((rows, row_tile), lambda i, s: (0, i)))
        args.append(in_hbm(acc))
    total = 0
    for g, pieces in enumerate(groups):
        span = sum(piece.shape[1] for piece in pieces)
        total += span
        in_specs += [pl.BlockSpec(piece.shape, lambda i, s: (0, 0)) for piece in pieces]
        in_specs.append(
            pl.BlockSpec(
                (pl.Element(row_tile), pl.Element(span)),
                lambda i, s, g=g: (i * row_tile, s[g] * 128),
            )
        )
        args += [*pieces, weight]
    return call(
        functools.partial(grad_body, [len(pieces) for pieces in groups], acc is not None),
        at,
        (depth // row_tile,),
        in_specs,
        [pl.BlockSpec((rows, row_tile), lambda i, s: (0, i))],
        [pltpu.HBM((rows, depth), F32)],
        2 * rows * depth * total,
        2 * depth * total + 8 * rows * depth,
        None,
        after=after,
        vmem=44,
        token=True,
    )(table, *args)


def last_body(group, counts, idx, acc, q, *refs):
    *refs, g_out, r_out, held, sems = refs
    i = pl.program_id(0)
    wide = held.shape[2]
    steps = held.shape[0]

    def fetch(n):
        start = pl.multiple_of((idx[0] * steps + n) * wide, wide)
        return pltpu.make_async_copy(acc.at[:, pl.ds(start, wide)], held.at[n], sems.at[n])

    @pl.when(i == 0)
    def _():
        for n in range(steps):
            fetch(n).start()

    t = None
    for count in counts:
        w, lo = refs[count], 0
        for piece in refs[:count]:
            hi = lo + piece.shape[1]
            u = dot(piece[...], w[:, lo:hi], NT)
            t = u if t is None else t + u
            lo = hi
        refs = refs[count + 1 :]
    fetch(i).wait()
    t = held[i] if t is None else t + held[i]
    g = t.astype(BF16)
    g_out[...] = g
    for i in range(group):
        r_out[i] = dot(q[:, cut(i)], g[:, cut(i)], TN).astype(BF16)


def grad_last(table, at, acc, q, groups, weight, half_heads, after=()):
    rows = acc.shape[0]
    group = group_of(half_heads)
    steps = half_heads // group
    wide = group * DH
    mine = pl.BlockSpec((rows, wide), lambda i, s: (0, s[0] * steps + i))
    in_specs, total = [pl.BlockSpec(memory_space=pltpu.HBM), mine], 0
    args = [in_hbm(acc), q]
    for n, pieces in enumerate(groups):
        span = sum(piece.shape[1] for piece in pieces)
        total += span
        in_specs += [pl.BlockSpec(piece.shape, lambda i, s: (0, 0)) for piece in pieces]
        in_specs.append(
            pl.BlockSpec(
                (pl.Element(wide), pl.Element(span)),
                lambda i, s, n=n: ((s[0] * steps + i) * wide, s[1 + n] * 128),
            )
        )
        args += [*pieces, weight]
    return call(
        functools.partial(last_body, group, [len(pieces) for pieces in groups]),
        at,
        (steps,),
        in_specs,
        [
            pl.BlockSpec((rows, wide), lambda i, s: (0, i)),
            pl.BlockSpec((group, DH, DH), lambda i, s: (i, 0, 0)),
        ],
        [pltpu.HBM((rows, half_heads * DH), BF16), sds((half_heads, DH, DH), BF16)],
        2 * rows * half_heads * DH * (total + DH),
        half_heads * DH * (rows * 8 + 2 * total),
        after=after,
        vmem=44,
        scratch=[
            pltpu.VMEM((steps, rows, wide), F32),
            pltpu.SemaphoreType.DMA((steps,)),
        ],
    )(table, *args)


def back_body(group, block, scale, extra, idx, q, k, v, g, state, *refs):
    dq, dk, dv = refs[extra:]
    mask = lower_mask(block)
    n = q.shape[0] // block
    for i in range(group):
        c = cut(i)
        before = state[i].astype(F32)
        later = None
        dks, dvs = [], []
        for b in range(n):
            r = slice(b * block, (b + 1) * block)
            qb, kb, vb, gb = q[r, c], k[r, c], v[r, c], g[r, c]
            gs = jnp.where(mask, dot(gb, vb, NT), 0.0).astype(BF16)
            s = jnp.where(mask, dot(qb, kb, NT), 0.0).astype(BF16)
            dq[r, c] = scale * (dot(gs, kb) + dot(gb, before.astype(BF16), NT))
            dks.append(dot(gs, qb, TN))
            dvs.append(dot(s, gb, TN))
            if b < n - 1:
                before = before + dot(kb, vb, TN)
        for b in reversed(range(n)):
            r = slice(b * block, (b + 1) * block)
            qb, kb, vb, gb = q[r, c], k[r, c], v[r, c], g[r, c]
            dkb, dvb = dks[b], dvs[b]
            if later is not None:
                lb = later.astype(BF16)
                dkb = dkb + dot(vb, lb, NT)
                dvb = dvb + dot(kb, lb)
            dk[r, c] = dkb.astype(dk.dtype)
            dv[r, c] = dvb.astype(dv.dtype)
            if b > 0:
                qg = dot(qb, gb, TN)
                later = qg if later is None else later + qg


def back_local(table, at, pairs, scale, q, k, v, g, state, filled, half_heads, after):
    rows, width = q.shape
    block = math.gcd(rows, 256)
    group = math.gcd(half_heads, 2)
    first, steps = pairs[0], pairs[1] - pairs[0]
    heads = group * steps
    wide = group * DH
    mine = pl.BlockSpec((rows, wide), lambda i, s: (0, s[0] * (half_heads // group) + first + i))
    own = pl.BlockSpec((rows, wide), lambda i, s: (0, first + i))
    extra = len(filled)
    half = pltpu.HBM((rows, half_heads * DH), BF16)
    return call(
        functools.partial(back_body, group, block, scale, extra),
        at,
        (steps,),
        [
            mine,
            mine,
            mine,
            own,
            pl.BlockSpec((group, DH, DH), lambda i, s: (first + i, 0, 0)),
        ]
        + [pl.BlockSpec(memory_space=pl.ANY)] * extra,
        [mine, own, own],
        [pltpu.HBM((rows, width), F32), half, half],
        2 * rows * DH * (5 * block + 4 * DH) * heads,
        rows * DH * heads * 20,
        {6 + n: n for n in range(extra)},
        after=after,
        vmem=30,
        token=True,
    )(table, in_hbm(q), in_hbm(k), in_hbm(v), in_hbm(g), state, *filled)


def later_body(heads, scale, extra, idx, k, v, later, dk_in, dv_in, *refs):
    dk, dv = refs[extra:]
    for i in range(heads):
        c = cut(i)
        dk[:, c] = scale * (dk_in[:, c] + dot(v[:, c], later[i], NT))
        dv[:, c] = scale * (dv_in[:, c] + dot(k[:, c], later[i]))


def add_later(table, at, scale, k, v, later, dk, dv, filled, half_heads, after):
    rows, width = k.shape
    block = math.gcd(rows, 256)
    wide = half_heads * DH
    mine = pl.BlockSpec((block, wide), lambda i, s: (i, s[0]))
    own = pl.BlockSpec((block, wide), lambda i, s: (i, 0))
    extra = len(filled)
    return call(
        functools.partial(later_body, half_heads, scale, extra),
        at,
        (rows // block,),
        [mine, mine, pl.BlockSpec((half_heads, DH, DH), lambda i, s: (0, 0, 0)), own, own]
        + [pl.BlockSpec(memory_space=pl.ANY)] * extra,
        [mine, mine],
        [sds((rows, width), F32)] * 2,
        4 * rows * DH * DH * half_heads,
        rows * DH * half_heads * 20,
        {6 + n: n for n in range(extra)},
        after=after,
        vmem=24,
    )(table, k, v, later, dk, dv, *filled)


def tie(array, *others):
    return lax.optimization_barrier((array,) + others)


def swap(array, axis, bit):
    size = lax.axis_size(axis)
    return lax.ppermute(array, axis, [(i, i ^ (1 << bit)) for i in range(size)])


def scan_states(theirs, mine, ctx_bits, flipped, fill):
    chunks = range(len(mine))
    pos = lax.axis_index("ctx")
    if flipped:
        pos = lax.axis_size("ctx") - 1 - pos
    held = []

    def beside(step, sent):
        got = [swap(array, "ctx", step) for array in sent]
        for n in chunks:
            done = fill[step, n]([sent[n], *held]) if (step, n) in fill else held
            got[n], *held[:] = tie(got[n], *done)
        return [array.astype(F32) for array in got]

    got = beside(0, theirs)
    own = [array.astype(F32) for array in mine]
    total = [own[n] + got[n] for n in chunks]
    prefix = [jnp.zeros_like(array) for array in total]
    for bit in range(1, ctx_bits):
        other = beside(bit, [array.astype(BF16) for array in total])
        before = (pos >> bit) & 1 == 1
        prefix = [prefix[n] + jnp.where(before, other[n], 0.0) for n in chunks]
        total = [total[n] + other[n] for n in chunks]
    upper = pos & 1 == 1
    mine_prefix = [(prefix[n] + jnp.where(upper, got[n], 0.0)).astype(BF16) for n in chunks]
    crossed = []
    for n in chunks:
        sent = (prefix[n] + jnp.where(upper, 0.0, own[n])).astype(BF16)
        if crossed:
            sent, crossed[-1], *held[:] = tie(sent, crossed[-1], *held)
        crossed.append(swap(sent, "ctx", 0))
        if (ctx_bits, n) in fill:
            held[:] = fill[ctx_bits, n]([sent, *held])
    return mine_prefix, crossed, held


def cuts_of(tiles, sizes):
    ends, at = [], 0
    for size in sizes:
        at = min(at + size, tiles)
        ends.append(at)
    ends[-1] = tiles
    starts = [0] + ends[:-1]
    return [(lo, hi) for lo, hi in zip(starts, ends) if lo < hi]


def on_device(queries, keys, values, teacher, out_weight, valid):
    rows, width = queries.shape
    heads = width // DH
    half_heads = heads // 2
    ctx_size = lax.axis_size("ctx")
    ctx_bits = ctx_size.bit_length() - 1
    chips = lax.axis_size("head") // 2
    ctx_id, head_id = lax.axis_index("ctx"), lax.axis_index("head")
    chip, core = head_id // 2, head_id % 2
    scale = 1.0 / math.sqrt(DH * rows * ctx_size)
    piece_width = teacher.shape[1]
    tile = 256 if piece_width % 256 == 0 else 128
    tiles = piece_width // tile
    sum_spans = [(lo * tile, hi * tile) for lo, hi in cuts_of(tiles, (2, 2, 1))]
    error_spans = [(lo * tile, hi * tile) for lo, hi in cuts_of(tiles, (3, 2))]

    my_half = ctx_id & 1
    entries = [my_half, 1 - my_half]
    for by in range(chips):
        for of_core in (core, 1 - core):
            device = lax.rem(chip + by, chips) * 2 + of_core
            entries.append(device * (piece_width // 128))
    table = [entry.astype(jnp.int32)[None] for entry in entries]
    mine_ix, theirs_ix = (0, 0), (1, 0)

    def column(by, crossed, lo):
        return 2 + 2 * (by % chips) + crossed, lo // 128


    chunks = 2 if half_heads % 2 == 0 else 1
    chunk_heads = half_heads // chunks
    last_step = ctx_bits - 1

    kv_theirs = kv_states(table, [theirs_ix], keys, values, chunk_heads, chunks)
    kv_mine = kv_states(table, [mine_ix], keys, values, chunk_heads, chunks, [kv_theirs[0]])
    parts, counts = {}, {}

    def intra_of(name, half):
        def run(after):
            parts[name], token = intra(
                table, [half], queries, keys, values, half_heads, after
            )
            return [token]

        return run

    def first_fill(after):
        counts["own"], *after = tie(jnp.full((8, 128), jnp.sum(valid), jnp.int32), *after)
        got = swap(counts["own"], "ctx", 0)
        after = intra_of("mine", mine_ix)(after)
        got, *after = tie(got, *after)
        counts["pair"] = counts["own"] + got
        if last_step > 1:
            counts["got"] = swap(counts["pair"], "ctx", 1)
        return after

    def last_fill(after):
        if "own" not in counts:
            after = first_fill(after)
        after = intra_of("theirs", theirs_ix)(after)
        count = counts["pair"]
        for bit in range(1, last_step):
            got = counts["got"] if bit == 1 else swap(count, "ctx", bit)
            got, *after = tie(got, *after)
            count = count + got
        return [*after, count]

    if chunks > 1:
        fill = {(last_step, 0): first_fill, (ctx_bits, 0): last_fill}
    else:
        fill = {(last_step, 0): last_fill}
    before_mine, before_theirs, (*held, count) = scan_states(
        kv_theirs, kv_mine, ctx_bits, False, fill
    )
    count = count + swap(count, "ctx", last_step)
    before_theirs[-1], count = tie(before_theirs[-1], count)
    other_weight = swap(out_weight, "head", 0)

    def both_cores(array):
        return array, swap(array, "head", 0)

    attn_mine = both_cores(
        attend(table, [mine_ix], scale, queries, parts["mine"], before_mine)
    )
    attn_theirs = both_cores(
        attend(table, [theirs_ix], scale, queries, parts["theirs"], before_theirs, held)
    )

    def terms(by, lo, hi, after=()):
        at = [mine_ix, theirs_ix, column(by, 0, lo)]
        return project(
            table, at, attn_mine, attn_theirs, out_weight, other_weight, hi - lo, after
        )

    def shift(array, by):
        size = 2 * chips
        return lax.ppermute(array, "head", [(i, (i + 2 * by) % size) for i in range(size)])

    arrived, own, after = [], [], []
    first = sum_spans[0][1]
    for n, (lo, hi) in enumerate(sum_spans):
        got = []
        if n == 1:
            own.append(terms(0, 0, first, after))
            after = [own[0]]
        if n == 2:
            after = after + arrived[0]
        for by in range(1, chips):
            summed = terms(by, lo, hi, after)
            after = [summed]
            got.append(shift(summed, by))
        arrived.append(got)
    if first < piece_width:
        own.append(terms(0, first, piece_width, after))
    else:
        own.append(terms(0, 0, piece_width, after))
    own_spans = [(0, first), (first, piece_width)] if len(own) > 1 else [(0, piece_width)]

    factor = rows * ctx_size / count[0, 0].astype(F32)
    weigh = (valid.astype(F32) * factor)[:, None]

    def columns(pieces, spans, lo, hi):
        inside = [
            piece[:, max(lo - base, 0) : hi - base].astype(F32)
            for (base, end), piece in zip(spans, pieces)
            if base < hi and lo < end
        ]
        return jnp.concatenate(inside, 1)

    def error_of(lo, hi):
        predicted = columns(own, own_spans, lo, hi)
        for by in range(1, chips):
            predicted = predicted + columns([got[by - 1] for got in arrived], sum_spans, lo, hi)
        return (weigh * (predicted - teacher[:, lo:hi].astype(F32))).astype(BF16)

    errors = [error_of(lo, hi) for lo, hi in error_spans]
    near = [errors, [swap(error, "head", 0) for error in errors]]
    states = {
        "theirs": jnp.concatenate(before_theirs),
        "mine": jnp.concatenate(before_mine),
    }
    acc, summed_near = grad_accumulate(
        table, [column(0, 0, 0), column(0, 1, 0)], near, None, out_weight, list(states.values())
    )

    early = max(1, len(error_spans) - 1)
    gathered = [[shift(error, by) for by in range(1, chips)] for error in errors]

    def sources(select, token, lo):
        groups, at = [], []
        for by in range(1, chips):
            pieces = [got[by - 1] for got in gathered[select]]
            *late, token = tie(pieces[0], *pieces[1:], token)
            groups += [pieces, [swap(piece, "head", 0) for piece in late]]
            at += [column(chips - by, 0, lo), column(chips - by, 1, lo)]
        return groups, at, token

    last, last_at, token = [], [], summed_near
    if chips > 1:
        far, at, token = sources(slice(0, early), summed_near, 0)
        acc, summed_far = grad_accumulate(table, at, far, acc, out_weight, [token])
        last, last_at, token = sources(slice(early, None), summed_far, error_spans[early][0])

    def last_of(half, after=()):
        return grad_last(table, [half, *last_at], acc, queries, last, out_weight, half_heads, after)

    g_theirs, r_theirs = last_of(theirs_ix, [token])
    g_mine, r_mine = last_of(mine_ix, [r_theirs])
    done_q, done_kv = [], {"theirs": [], "mine": []}
    halves = {"theirs": (theirs_ix, g_theirs), "mine": (mine_ix, g_mine)}

    def back(name, lo, hi, after):
        half, g = halves[name]
        *got, token = back_local(
            table, [half], (lo, hi), scale, queries, keys, values, g, states[name],
            done_q + done_kv[name], half_heads, after,
        )
        done_q[:], done_kv[name] = got[:1], got[1:]
        return [token]

    groups = half_heads // math.gcd(half_heads, 2)
    split = max(1, groups * 3 // 4)
    order = [("mine", split, groups), ("mine", 0, split), ("theirs", 0, groups)]

    def beside_backward(step):
        def run(after):
            if step == 0:
                after = [r_mine]
            todo = order[:1]
            del order[:1]
            for name, lo, hi in todo:
                if lo < hi:
                    after = back(name, lo, hi, after)
            return after

        return run

    (later_mine,), (later_theirs,), token = scan_states(
        [r_theirs], [r_mine], ctx_bits, True,
        {(n, 0): beside_backward(n) for n in range(ctx_bits)},
    )
    token = [*token, later_mine]
    for name, lo, hi in order:
        if lo < hi:
            token = back(name, lo, hi, token)
    (q_grad,) = done_q
    grads = add_later(
        table, [mine_ix], scale, keys, values, later_mine, *done_kv["mine"], [], half_heads, token
    )
    k_grad, v_grad = add_later(
        table, [theirs_ix], scale, keys, values, later_theirs, *done_kv["theirs"], list(grads),
        half_heads, [],
    )
    return q_grad, k_grad, v_grad


def solution(mesh):
    in_specs = (
        P("ctx", "head"),
        P("ctx", "head"),
        P("ctx", "head"),
        P("ctx", "head"),
        P("head", None),
        P("ctx"),
    )
    out_specs = (P("ctx", "head"), P("ctx", "head"), P("ctx", "head"))
    return jax.shard_map(
        on_device, mesh=mesh, in_specs=in_specs, out_specs=out_specs, check_vma=False
    )
```
